32 devices in a mesh: pairs: 2 (over x), rows: 8 (over z, y), cols: 2 (over core).
Axes of the slice: x: 2, y: 2, z: 4, core: 2. Of those that a mesh axis runs over, the one named last changes fastest.
Arguments:
- left_feat: bfloat16 [32, 512, 256], P(('pairs', 'rows'), 'cols'), parts along dimension 0, may hold values from -6 to 6
- right_feat: bfloat16 [32, 512, 256], P(('pairs', 'rows'), 'cols'), parts along dimension 0, may hold values from -6 to 6
- block_list: int32 [16, 8, 2], P(('pairs', 'rows'), 'cols'), parts along dimension 0, may hold values from 0 to 1, as said below
- block_count: int32 [16, 8], P(('pairs', 'rows'), 'cols'), parts along dimension 0, may hold values from 1 to 2
- spatial_first: bfloat16 [3, 3, 16, 16], replicated, may hold values from -0.75 to 0.75
- spatial_second: bfloat16 [3, 3, 16, 16], replicated, may hold values from -0.75 to 0.75
- disparity_weight: bfloat16 [17, 16], replicated, may hold values from -0.5 to 0.5
Outputs:
- cost: float32 [32, 512, 256], P(('pairs', 'rows'), 'cols'), parts along dimension 0
The draws below stay inside these ranges and needn't reach their ends.
There are 2 independent parts, one for each index of `pairs`. The reference program is written for one: setup_inputs(seed, part) draws one part's arguments, and reference() takes and returns one part's arrays. A program takes and returns all parts, laid end to end along the dimension named above; an argument that names none is the same for every part. Nothing has to cross between parts.
Inputs may be any that keep to these rules, and one draw needn't show every extreme that they name: `block_list`: for each tile the 2 entries are different block numbers; entries in slots at or past the tile's block_count are not listed.
All inputs are finite; a program needn't handle non-finite values.
Results may differ from the reference program's by a relative error of at most 0.0059.
Values may be sent and summed in bfloat16 or wider, within the bound.
No kernel may reach another device: no remote copies, remote signals or barrier semaphores. Data moves between devices by JAX's collectives and lax.ppermute only.
A program may use at most 128 MiB of HBM per device.

```python
import jax
import jax.numpy as jnp
from jax import lax

C = 256
G = 16
DB = 128
NBLK = 2
MAXB = 2
TILE = 64
TAPS = 17
TR = 2
BANDS = 8
H = 16
W = 512
TILES = 8
NDISP = 256


def draw_block_list(key, part):
    key = jax.random.fold_in(key, 11)
    scores = jax.random.randint(key, (BANDS, TILES, NBLK), 0, 1 << 20)
    scores = scores * NBLK + jnp.arange(NBLK, dtype=jnp.int32)
    ordering = jnp.argsort(scores, axis=-1, stable=True).astype(jnp.int32)
    return ordering[..., :MAXB]


def draw_block_count(key, part):
    key = jax.random.fold_in(key, 23)
    return jax.random.randint(key, (BANDS, TILES), 1, MAXB + 1).astype(jnp.int32)


def block_scale(rng, dims, cuts, least, largest):
    def one(dim, parts):
        heights = jax.random.uniform(jax.random.fold_in(jax.random.fold_in(rng, 6), dim), (parts,), jnp.float32, least / len(cuts), largest / len(cuts))
        return jnp.repeat(jnp.exp(heights), dims[dim] // parts).reshape((-1,) + (1,) * (len(dims) - dim - 1))

    loudness = one(*cuts[0])
    for cut in cuts[1:]:
        loudness = loudness * one(*cut)
    return loudness


def gaussian(own_key, extent, deviation, bound, shards=(), held_as=jnp.bfloat16):
    loudness = block_scale(own_key, extent, shards, -0.22, 0.18) if shards else 1.0
    array = jax.random.normal(own_key, extent, jnp.float32) * deviation * loudness
    return jnp.minimum(jnp.maximum(array, -bound), bound).astype(held_as)


def setup_inputs(seed: int = 0, part: int = 0) -> dict:
    seeds = jax.random.split(jax.random.key(seed), 8)
    part_splits = jax.random.split(jax.random.fold_in(seeds[7], part), 8)
    return {
        "left_feat": gaussian(part_splits[0], (H, W, C), 1.0, 6.0, ((0, 8), (1, 2))),
        "right_feat": gaussian(part_splits[1], (H, W, C), 1.0, 6.0, ((0, 8), (1, 2))),
        "block_list": draw_block_list(jax.random.fold_in(jax.random.fold_in(seeds[7], part), 71), part),
        "block_count": draw_block_count(jax.random.fold_in(jax.random.fold_in(seeds[7], part), 71), part),
        "spatial_first": gaussian(seeds[4], (3, 3, G, G), (9 * G // 2) ** -0.5, 0.75),
        "spatial_second": gaussian(seeds[5], (3, 3, G, G), (9 * G // 2) ** -0.5, 0.75),
        "disparity_weight": gaussian(seeds[6], (TAPS, G), (TAPS * G // 2) ** -0.5, 0.5),
    }


def skew_band(products):
    pixel_count = products.shape[-2]
    window_len = products.shape[-1]
    block_len = window_len - pixel_count
    leading = products.shape[:-2]
    flattened = products.reshape(leading + (pixel_count * window_len,))
    flattened = jnp.pad(flattened, [(0, 0)] * len(leading) + [(0, pixel_count)])
    skewed = flattened.reshape(leading + (pixel_count, window_len + 1))
    return skewed[..., 1:block_len + 1][..., ::-1]


def group_products(left_piece, right_window):
    row_count, pixel_count, channels = left_piece.shape
    window_len = right_window.shape[1]
    left_groups = left_piece.astype(jnp.float32).reshape(row_count, pixel_count, G, channels // G)
    right_groups = right_window.astype(jnp.float32).reshape(row_count, window_len, G, channels // G)
    products = jnp.einsum("yigc,yjgc->gyij", left_groups, right_groups, precision=lax.Precision.HIGHEST)
    return skew_band(products)


def spatial_same(volume, kernel):
    return lax.conv_general_dilated(volume.astype(jnp.float32), kernel.astype(jnp.float32), (1, 1), ((1, 1), (1, 1)), dimension_numbers=("CHWN", "HWOI", "CHWN"), precision=lax.Precision.HIGHEST)


def disparity_conv(lower_rim, middle, upper_rim, kernel):
    extended = jnp.concatenate([lower_rim, middle, upper_rim], axis=3).astype(jnp.float32)
    weights = kernel.astype(jnp.float32)[None, :, :, None]
    result = lax.conv_general_dilated(extended, weights, (1, 1), "VALID", dimension_numbers=("CHNW", "HWIO", "CHNW"), precision=lax.Precision.HIGHEST)
    return result[0]


def reference(left_feat, right_feat, block_list, block_count, spatial_first, spatial_second, disparity_weight):
    height, breadth, channels = left_feat.shape
    slot_ids = jnp.arange(block_list.shape[2], dtype=jnp.int32)
    live = slot_ids[None, None, :] < block_count[:, :, None]
    block_ids = jnp.arange(NBLK, dtype=jnp.int32)
    hits = (block_list[..., None] == block_ids) & live[..., None]
    active = jnp.any(hits, axis=2).astype(jnp.float32)
    pixel_mask = jnp.repeat(jnp.repeat(active, TR, axis=0), TILE, axis=1)
    right_padded = jnp.pad(right_feat, ((0, 0), (NDISP, 0), (0, 0)))
    corr_scale = (C // G) ** -0.5
    half_taps = TAPS // 2
    lower_rim = jnp.zeros((G, height, breadth, half_taps), jnp.bfloat16)
    current = None
    results = []
    for block_index in range(NBLK):
        def tile_piece(tile_index):
            start = tile_index * TILE
            left_piece = lax.dynamic_slice_in_dim(left_feat, start, TILE, 1)
            right_window = lax.dynamic_slice_in_dim(right_padded, start - block_index * DB - DB + NDISP, TILE + DB, 1)
            return group_products(left_piece, right_window)

        tiles = lax.map(tile_piece, jnp.arange(breadth // TILE, dtype=jnp.int32))
        products = jnp.moveaxis(tiles, 0, 2).reshape(G, height, breadth, DB)
        correlation = (products * corr_scale * pixel_mask[:, :, block_index][None, :, :, None]).astype(jnp.bfloat16)
        first_hidden = jax.nn.relu(spatial_same(correlation, spatial_first)).astype(jnp.bfloat16)
        newest = jax.nn.relu(spatial_same(first_hidden, spatial_second)).astype(jnp.bfloat16)
        if current is not None:
            results.append(disparity_conv(lower_rim, current, newest[..., :half_taps], disparity_weight))
            lower_rim = current[..., DB - half_taps:]
        current = newest
    upper_zero = jnp.zeros((G, height, breadth, half_taps), jnp.bfloat16)
    results.append(disparity_conv(lower_rim, current, upper_zero, disparity_weight))
    return jnp.concatenate(results, axis=-1)
```

```python
import functools

import jax
import jax.numpy as jnp
import numpy as np
from jax import lax
from jax.experimental import pallas as pl
from jax.experimental.pallas import tpu as pltpu
from jax.sharding import PartitionSpec as P

G = 16
DB = 128
NBLK = 2
TILE = 64
TAPS = 17
BF = jnp.bfloat16
F32 = jnp.float32
NT = (((1,), (1,)), ((), ()))


def shifted(x, axis, by):
    count = lax.axis_size(axis)
    pairs = [(i, i + by) for i in range(count) if 0 <= i + by < count]
    return lax.ppermute(x, axis, pairs)


def toeplitz(weights, out_cols, out_rows, order):
    in_cols, in_rows = out_cols + 2, out_rows + 2
    pick = np.zeros((out_cols, out_rows, in_cols, in_rows, 3, 3), np.float32)
    for xo in range(out_cols):
        for yo in range(out_rows):
            for i in range(3):
                for j in range(3):
                    pick[xo, yo, xo + j, yo + i, i, j] = 1.0
    pick = pick.reshape(-1, 9).astype(BF)
    flat = weights.reshape(9, G * G)
    full = jnp.dot(pick, flat, preferred_element_type=F32).astype(BF)
    full = full.reshape(out_cols, out_rows, in_cols, in_rows, G, G)
    full = full.transpose(order + (2, 3, 5))
    return full.reshape(out_cols * out_rows * G, in_cols * in_rows * G)


def banded(weights, ndisp):
    e = lax.broadcasted_iota(jnp.int32, (G, ndisp, ndisp), 1)
    d = lax.broadcasted_iota(jnp.int32, (G, ndisp, ndisp), 2)
    tap = ndisp - 1 - e - d + TAPS // 2
    out = jnp.zeros((G, ndisp, ndisp), BF)
    for k in range(TAPS):
        out = jnp.where(tap == k, weights[k][:, None, None], out)
    return out.reshape(G * ndisp, ndisp)


def kernel(
    edge_ref, up, own, dn, up_n, own_n, dn_n, w1, w2, tm, out_ref,
    corr, hidden, second, left_zero, masks,
    *, cols, ndisp,
):
    channels = own.shape[1]
    is_left = edge_ref[2] == 1
    is_right = edge_ref[3] == 1
    group_of = lax.broadcasted_iota(jnp.int32, (G, channels), 1) // (channels // G)
    gmask = jnp.where(
        group_of == lax.broadcasted_iota(jnp.int32, (G, channels), 0), (channels // G) ** -0.5, 0.0
    ).astype(F32)
    lane = lax.broadcasted_iota(jnp.int32, (G, ndisp), 1)
    rows = 6

    def put(xx, y, value):
        start = pl.multiple_of((xx * rows + y) * G, G)
        corr[pl.ds(start, G), :] = value

    def spread(lines):
        lines = lines.astype(F32)
        return jnp.concatenate(
            [(lines[i : i + 1, :] * gmask).astype(BF) for i in range(lines.shape[0])], axis=0
        )

    for band, (b, n) in enumerate(((up, up_n), (own, own_n), (dn, dn_n))):
        masks[...] = b[4 * cols : 4 * cols + 16, :].astype(F32)
        mask_n = n[4 * cols : 4 * cols + 16, :].astype(F32)
        for yb in range(2):
            y = 2 * band + yb
            r_own = (2 + yb) * cols
            left_zero[...] = jnp.where(is_left, jnp.zeros((), BF), n[r_own : r_own + cols, :])

            def block(k, carry, b=b, yb=yb, y=y, r_own=r_own):
                x0 = k * 16
                lines = b[pl.ds(pl.multiple_of(yb * cols + x0, 16), 16), :]
                a = spread(lines)
                hi = lax.dot_general(a, b[r_own : r_own + cols, :], NT, preferred_element_type=F32)
                lo = lax.dot_general(a, left_zero[...], NT, preferred_element_type=F32)
                m = masks[pl.ds(k, 1), :]
                for i in range(16):
                    x = x0 + i
                    s = jnp.where(lane <= x, hi[i * G : i * G + G], lo[i * G : i * G + G])
                    s = pltpu.roll(s, ndisp - 1 - x, 1)
                    put(x + 2, y, (s * m).astype(BF))
                return carry

            lax.fori_loop(0, cols // 16, block, 0)

            tail = n[yb * cols + cols - 16 : yb * cols + cols, :][14:16]
            head = n[yb * cols : yb * cols + 16, :][0:2]
            a = spread(jnp.concatenate([tail, head], axis=0))
            p_n = lax.dot_general(a, n[r_own : r_own + cols, :], NT, preferred_element_type=F32)
            p_o = lax.dot_general(a, b[r_own : r_own + cols, :], NT, preferred_element_type=F32)
            m_l = jnp.where(is_left, 0.0, mask_n[15:16])
            m_r = jnp.where(is_right, 0.0, mask_n[0:1])
            s = jnp.where(lane <= ndisp - 2, p_n[0:G], 0.0)
            put(0, y, (pltpu.roll(s, 1, 1) * m_l).astype(BF))
            put(1, y, (p_n[G : 2 * G] * m_l).astype(BF))
            s = jnp.where(lane <= 0, p_n[2 * G : 3 * G], p_o[2 * G : 3 * G])
            put(cols + 2, y, (pltpu.roll(s, ndisp - 1, 1) * m_r).astype(BF))
            s = jnp.where(lane <= 1, p_n[3 * G : 4 * G], p_o[3 * G : 4 * G])
            put(cols + 3, y, (pltpu.roll(s, ndisp - 2, 1) * m_r).astype(BF))

    step1 = 3
    k1 = (step1 + 2) * rows * G
    m1 = step1 * 4 * G

    def first(s, carry):
        data = corr[pl.ds(pl.multiple_of(s * (step1 * rows * G), 16), k1), :]
        h = jnp.dot(w1[...], data, preferred_element_type=F32)
        hidden[pl.ds(pl.multiple_of(s * m1, 16), m1), :] = jnp.maximum(h, 0.0).astype(BF)
        return carry

    lax.fori_loop(0, (cols + 2) // step1, first, 0)

    zero = jnp.zeros((G, ndisp), BF)
    for which, row in ((0, 0), (1, 3)):
        @pl.when(edge_ref[which] == 1)
        def _():
            def clear(i, carry):
                hidden[pl.ds(pl.multiple_of((i * 4 + row) * G, G), G), :] = zero
                return carry

            lax.fori_loop(0, cols + 2, clear, 0)

    for which, col in ((2, 0), (3, cols + 1)):
        @pl.when(edge_ref[which] == 1)
        def _():
            hidden[col * 4 * G : (col + 1) * 4 * G, :] = jnp.zeros((4 * G, ndisp), BF)

    def next_hidden(u, carry):
        halves = []
        for v in range(2):
            start = pl.multiple_of((2 * u + v) * (8 * 4 * G), 16)
            data = hidden[pl.ds(start, 10 * 4 * G), :]
            h = jnp.dot(w2[...], data, preferred_element_type=F32)
            halves.append(jnp.maximum(h, 0.0))
        for y in range(2):
            for o in range(G):
                r = (y * G + o) * 8
                both = jnp.concatenate([halves[0][r : r + 8], halves[1][r : r + 8]], axis=0)
                second[y, pl.ds(pl.multiple_of(u * 16, 16), 16), o * ndisp : (o + 1) * ndisp] = (
                    both.astype(BF)
                )
        return carry

    lax.fori_loop(0, cols // 16, next_hidden, 0)

    for y in range(2):
        out_ref[y] = jnp.dot(second[y], tm[...], preferred_element_type=F32)


def tile_masks(block_list, block_count, cols, ndisp):
    slot_ids = jnp.arange(block_list.shape[2], dtype=jnp.int32)
    live = slot_ids[None, :] < block_count[0][:, None]
    block_ids = jnp.arange(NBLK, dtype=jnp.int32)
    hits = (block_list[0][..., None] == block_ids) & live[..., None]
    active = jnp.any(hits, axis=1)
    lane_block = (ndisp - 1 - jnp.arange(ndisp)) // DB
    lanes = jnp.where(lane_block[None, :] == 0, active[:, :1], active[:, 1:2])
    return jnp.repeat(lanes.astype(BF), TILE // 16, axis=0)


def body(
    left_feat, right_feat, block_list, block_count, spatial_first, spatial_second, disparity_weight
):
    row_count, cols, channels = left_feat.shape
    ndisp = NBLK * DB
    masks = tile_masks(block_list, block_count, cols, ndisp)
    pack = jnp.concatenate(
        [left_feat.reshape(-1, channels), right_feat.reshape(-1, channels), masks], axis=0
    )
    up = shifted(pack, "rows", 1)
    dn = shifted(pack, "rows", -1)
    swap = [(0, 1), (1, 0)]
    own_n = lax.ppermute(pack, "cols", swap)
    up_n = lax.ppermute(up, "cols", swap)
    dn_n = lax.ppermute(dn, "cols", swap)
    row = lax.axis_index("rows")
    col = lax.axis_index("cols")
    edges = jnp.stack(
        [row == 0, row == lax.axis_size("rows") - 1, col == 0, col == lax.axis_size("cols") - 1]
    ).astype(jnp.int32)
    w1 = toeplitz(spatial_first, 3, 4, (0, 1, 4))
    w2 = toeplitz(spatial_second, 8, 2, (1, 4, 0))
    tm = banded(disparity_weight, ndisp)
    vmem = pl.BlockSpec(memory_space=pltpu.VMEM)
    return pl.pallas_call(
        functools.partial(kernel, cols=cols, ndisp=ndisp),
        out_shape=jax.ShapeDtypeStruct((row_count, cols, ndisp), F32),
        in_specs=[pl.BlockSpec(memory_space=pltpu.SMEM)] + [vmem] * 9,
        out_specs=vmem,
        scratch_shapes=[
            pltpu.VMEM(((cols + 4) * 6 * G, ndisp), BF),
            pltpu.VMEM(((cols + 2) * 4 * G, ndisp), BF),
            pltpu.VMEM((2, cols, G * ndisp), BF),
            pltpu.VMEM((cols, channels), BF),
            pltpu.VMEM((16, ndisp), F32),
        ],
        compiler_params=pltpu.CompilerParams(vmem_limit_bytes=56 * 1024 * 1024),
    )(edges, up, pack, dn, up_n, own_n, dn_n, w1, w2, tm)


def solution(mesh):
    in_specs = (
        P(("pairs", "rows"), "cols", None),
        P(("pairs", "rows"), "cols", None),
        P(("pairs", "rows"), "cols", None),
        P(("pairs", "rows"), "cols"),
        P(),
        P(),
        P(),
    )
    out_specs = P(("pairs", "rows"), "cols", None)
    return jax.shard_map(body, mesh=mesh, in_specs=in_specs, out_specs=out_specs, check_vma=False)
```

```python
import functools

import jax
import jax.numpy as jnp
from jax import lax
from jax.experimental import pallas as pl
from jax.experimental.pallas import tpu as pltpu
from jax.sharding import PartitionSpec as P

G = 16
DB = 128
NBLK = 2
TILE = 64
TAPS = 17
BF = jnp.bfloat16
F32 = jnp.float32
NT = (((1,), (1,)), ((), ()))


def shifted(x, axis, by):
    count = lax.axis_size(axis)
    pairs = [(i, i + by) for i in range(count) if 0 <= i + by < count]
    return lax.ppermute(x, axis, pairs)


def tap_row(weights, in_rows, width):
    taps = weights.transpose(2, 1, 0, 3)
    taps = jnp.pad(taps, ((0, 0), (0, 0), (0, in_rows - 3), (0, 0)))
    taps = taps.reshape(G, 3 * in_rows * G)
    return jnp.pad(taps, ((0, 0), (0, width - taps.shape[1]))).astype(F32)


def banded(weights, ndisp):
    e = lax.broadcasted_iota(jnp.int32, (G, ndisp, ndisp), 1)
    d = lax.broadcasted_iota(jnp.int32, (G, ndisp, ndisp), 2)
    tap = ndisp - 1 - e - d + TAPS // 2
    out = jnp.zeros((G, ndisp, ndisp), BF)
    for k in range(TAPS):
        out = jnp.where(tap == k, weights[k][:, None, None], out)
    return out.reshape(G * ndisp, ndisp)


def kernel(
    edge_ref, up, own, dn, up_n, own_n, dn_n, t1, t2, tm, out_ref,
    xs, xn, corr, hidden, second, left_zero, w1, w2, sems,
    *, cols, ndisp,
):
    channels = xs.shape[2]
    rows = 6
    is_left = edge_ref[2] == 1
    is_right = edge_ref[3] == 1
    copies = []
    for i, (src, dst) in enumerate(
        ((own, xs.at[1]), (own_n, xn.at[1]), (up, xs.at[0]), (up_n, xn.at[0]), (dn, xs.at[2]), (dn_n, xn.at[2]))
    ):
        copies.append(pltpu.make_async_copy(src, dst, sems.at[i]))
        copies[-1].start()

    wide1, wide2 = t1.shape[1], t2.shape[1]
    for xo in range(3):
        for yo in range(4):
            r = (xo * 4 + yo) * G
            moved = pltpu.roll(t1[...], (xo * 6 + yo) * G, 1)
            w1[r : r + G, :] = moved.astype(BF)[:, : w1.shape[1]]
    blocks = []
    for yo in range(2):
        for xo in range(8):
            by = (xo * 4 + yo) * G
            blocks.append((pltpu.roll(t2[...], by, 1) if by else t2[...]).astype(BF))
    plain = jnp.concatenate(blocks, axis=0)
    r = lax.broadcasted_iota(jnp.int32, (256, 256), 0)
    c = lax.broadcasted_iota(jnp.int32, (256, 256), 1)
    order = (r // 128) * 128 + (r % 8) * G + (r // 8) % G
    order = jnp.where(c == order, 1.0, 0.0).astype(BF)
    w2[...] = jnp.dot(order, plain, preferred_element_type=F32).astype(BF)

    for copy in copies:
        copy.wait()

    group_of = lax.broadcasted_iota(jnp.int32, (G, channels), 1) // (channels // G)
    gmask = jnp.where(
        group_of == lax.broadcasted_iota(jnp.int32, (G, channels), 0), (channels // G) ** -0.5, 0.0
    ).astype(F32)
    lane = lax.broadcasted_iota(jnp.int32, (G, ndisp), 1)

    def spread(lines):
        lines = lines.astype(F32)
        return jnp.concatenate(
            [(lines[i : i + 1, :] * gmask).astype(BF) for i in range(lines.shape[0])], axis=0
        )

    def corr_row(y, carry):
        band, yb = y // 2, y % 2

        def put(xx, value):
            corr[pl.ds(pl.multiple_of((xx * rows + y) * G, G), G), :] = value.astype(BF)

        def pixels(ref, x0, count):
            return ref[band, pl.ds(pl.multiple_of(yb * cols + x0, 16), count), :]

        r_start = pl.multiple_of((2 + yb) * cols, 16)
        near = xn[band, pl.ds(r_start, cols), :]
        left_zero[...] = jnp.where(is_left, jnp.zeros_like(near), near)
        masks = xs[band, 4 * cols : 4 * cols + 16, :].astype(F32)
        for k in range(cols // 16):
            x0 = k * 16
            a = spread(pixels(xs, x0, 16))
            hi = lax.dot_general(a, xs[band, pl.ds(r_start, cols), :], NT, preferred_element_type=F32)
            lo = lax.dot_general(a, left_zero[...], NT, preferred_element_type=F32)
            m = masks[k : k + 1]
            for i in range(16):
                x = x0 + i
                s = jnp.where(lane <= x, hi[i * G : i * G + G], lo[i * G : i * G + G])
                if x < ndisp - 1:
                    s = pltpu.roll(s, ndisp - 1 - x, 1)
                put(x + 2, s * m)

        mask_n = xn[band, 4 * cols : 4 * cols + 16, :].astype(F32)
        tail = pixels(xn, cols - 16, 16).astype(F32)[14:16]
        head = pixels(xn, 0, 16).astype(F32)[0:2]
        a = spread(jnp.concatenate([tail, head], axis=0))
        p_n = lax.dot_general(a, xn[band, pl.ds(r_start, cols), :], NT, preferred_element_type=F32)
        p_o = lax.dot_general(a, xs[band, pl.ds(r_start, cols), :], NT, preferred_element_type=F32)
        m_l = jnp.where(is_left, 0.0, mask_n[15:16])
        m_r = jnp.where(is_right, 0.0, mask_n[0:1])
        s = jnp.where(lane <= ndisp - 2, p_n[0:G], 0.0)
        put(0, pltpu.roll(s, 1, 1) * m_l)
        put(1, p_n[G : 2 * G] * m_l)
        s = jnp.where(lane <= 0, p_n[2 * G : 3 * G], p_o[2 * G : 3 * G])
        put(cols + 2, pltpu.roll(s, ndisp - 1, 1) * m_r)
        s = jnp.where(lane <= 1, p_n[3 * G : 4 * G], p_o[3 * G : 4 * G])
        put(cols + 3, pltpu.roll(s, ndisp - 2, 1) * m_r)
        return carry

    lax.fori_loop(0, rows, corr_row, 0)

    step1 = 3
    k1 = (step1 + 2) * rows * G
    m1 = step1 * 4 * G

    def first(s, carry):
        data = corr[pl.ds(pl.multiple_of(s * (step1 * rows * G), 16), k1), :]
        h = jnp.dot(w1[...], data, preferred_element_type=F32)
        hidden[pl.ds(pl.multiple_of(s * m1, 16), m1), :] = jnp.maximum(h, 0.0).astype(BF)
        return carry

    lax.fori_loop(0, -(-(cols + 2) // step1), first, 0, unroll=8)

    zero = jnp.zeros((G, ndisp), BF)
    for which, row in ((0, 0), (1, 3)):
        @pl.when(edge_ref[which] == 1)
        def _():
            def clear(i, carry):
                hidden[pl.ds(pl.multiple_of((i * 4 + row) * G, G), G), :] = zero
                return carry

            lax.fori_loop(0, cols + 2, clear, 0, unroll=8)

    for which, col in ((2, 0), (3, cols + 1)):
        @pl.when(edge_ref[which] == 1)
        def _():
            hidden[col * 4 * G : (col + 1) * 4 * G, :] = jnp.zeros((4 * G, ndisp), BF)

    def next_hidden(u, carry):
        halves = []
        for v in range(2):
            start = pl.multiple_of((2 * u + v) * (8 * 4 * G), 16)
            data = hidden[pl.ds(start, 10 * 4 * G), :]
            h = jnp.dot(w2[...], data, preferred_element_type=F32)
            halves.append(jnp.maximum(h, 0.0))
        for y in range(2):
            for o in range(G):
                r = (y * G + o) * 8
                both = jnp.concatenate([halves[0][r : r + 8], halves[1][r : r + 8]], axis=0)
                second[y, pl.ds(pl.multiple_of(u * 16, 16), 16), o * ndisp : (o + 1) * ndisp] = (
                    both.astype(BF)
                )
        return carry

    lax.fori_loop(0, cols // 16, next_hidden, 0, unroll=4)

    for y in range(2):
        out_ref[y] = jnp.dot(second[y], tm[...], preferred_element_type=F32)


def tile_masks(block_list, block_count, cols, ndisp):
    slot_ids = jnp.arange(block_list.shape[2], dtype=jnp.int32)
    live = slot_ids[None, :] < block_count[0][:, None]
    block_ids = jnp.arange(NBLK, dtype=jnp.int32)
    hits = (block_list[0][..., None] == block_ids) & live[..., None]
    active = jnp.any(hits, axis=1)
    lane_block = (ndisp - 1 - jnp.arange(ndisp)) // DB
    lanes = jnp.where(lane_block[None, :] == 0, active[:, :1], active[:, 1:2])
    return jnp.repeat(lanes.astype(BF), TILE // 16, axis=0)


def body(
    left_feat, right_feat, block_list, block_count, spatial_first, spatial_second, disparity_weight
):
    row_count, cols, channels = left_feat.shape
    ndisp = NBLK * DB
    masks = tile_masks(block_list, block_count, cols, ndisp)
    pack = jnp.concatenate(
        [left_feat.reshape(-1, channels), right_feat.reshape(-1, channels), masks], axis=0
    )
    up = shifted(pack, "rows", 1)
    dn = shifted(pack, "rows", -1)
    swap = [(0, 1), (1, 0)]
    own_n = lax.ppermute(pack, "cols", swap)
    up_n = lax.ppermute(up, "cols", swap)
    dn_n = lax.ppermute(dn, "cols", swap)
    row = lax.axis_index("rows")
    col = lax.axis_index("cols")
    edges = jnp.stack(
        [row == 0, row == lax.axis_size("rows") - 1, col == 0, col == lax.axis_size("cols") - 1]
    ).astype(jnp.int32)
    t1 = tap_row(spatial_first, 6, 512)
    t2 = tap_row(spatial_second, 4, 640)
    tm = banded(disparity_weight, ndisp)
    packed = pack.shape[0]
    steps1 = -(-(cols + 2) // 3)
    vmem = pl.BlockSpec(memory_space=pltpu.VMEM)
    hbm = pl.BlockSpec(memory_space=pl.ANY)
    return pl.pallas_call(
        functools.partial(kernel, cols=cols, ndisp=ndisp),
        out_shape=jax.ShapeDtypeStruct((row_count, cols, ndisp), F32),
        in_specs=[pl.BlockSpec(memory_space=pltpu.SMEM)] + [hbm] * 6 + [vmem] * 3,
        out_specs=vmem,
        scratch_shapes=[
            pltpu.VMEM((3, packed, channels), BF),
            pltpu.VMEM((3, packed, channels), BF),
            pltpu.VMEM(((steps1 * 3 + 2) * 6 * G, ndisp), BF),
            pltpu.VMEM((steps1 * 3 * 4 * G, ndisp), BF),
            pltpu.VMEM((2, cols, G * ndisp), BF),
            pltpu.VMEM((cols, channels), BF),
            pltpu.VMEM((3 * 4 * G, 5 * 6 * G), BF),
            pltpu.VMEM((8 * 2 * G, 10 * 4 * G), BF),
            pltpu.SemaphoreType.DMA((6,)),
        ],
        compiler_params=pltpu.CompilerParams(vmem_limit_bytes=56 * 1024 * 1024),
    )(edges, up, pack, dn, up_n, own_n, dn_n, t1, t2, tm)


def solution(mesh):
    in_specs = (
        P(("pairs", "rows"), "cols", None),
        P(("pairs", "rows"), "cols", None),
        P(("pairs", "rows"), "cols", None),
        P(("pairs", "rows"), "cols"),
        P(),
        P(),
        P(),
    )
    out_specs = P(("pairs", "rows"), "cols", None)
    return jax.shard_map(body, mesh=mesh, in_specs=in_specs, out_specs=out_specs, check_vma=False)
```

```python
import jax
import jax.numpy as jnp
from jax import lax
from jax.experimental import pallas as pl
from jax.experimental.pallas import tpu as pltpu
from jax.sharding import PartitionSpec as P

G = 16
DB = 128
NBLK = 2
TILE = 64
TAPS = 17
STEP1 = 6
STEP2 = 8
PAIR = 2 * G
BF = jnp.bfloat16
F32 = jnp.float32
NT = (((1,), (1,)), ((), ()))
VMEM = pl.BlockSpec(memory_space=pltpu.VMEM)
SMEM = pl.BlockSpec(memory_space=pltpu.SMEM)
HBM = pl.BlockSpec(memory_space=pl.ANY)
LIMIT = pltpu.CompilerParams(vmem_limit_bytes=36 * 1024 * 1024)


def cost(us):
    return pl.CostEstimate(flops=us * 10**9, bytes_accessed=us * 10**6, transcendentals=0)


def iota(shape, dim):
    return lax.broadcasted_iota(jnp.int32, shape, dim)


def place():
    row, col = lax.axis_index("rows"), lax.axis_index("cols")
    rows, cols = lax.axis_size("rows"), lax.axis_size("cols")
    return col == 0, col == cols - 1, row == 0, row == rows - 1, row % 2


def pack_kernel(left, right, block_list, block_count, p0, p1, sems):
    cols = left.shape[1]
    copies = []
    for c, p in enumerate((p0, p1)):
        for i, src in enumerate((left, right)):
            dst = p.at[pl.ds(i * cols, cols), :]
            copies.append(pltpu.make_async_copy(src.at[c], dst, sems.at[2 * c + i]))
            copies[-1].start()
    ndisp = p0.shape[1]
    lane_block = (ndisp - 1 - iota((TILE // 16, ndisp), 1)) // DB
    lines = []
    for tile in range(cols // TILE):
        line = jnp.zeros(lane_block.shape, F32)
        for slot in range(block_list.shape[1]):
            listed = jnp.where(slot < block_count[0, tile], block_list[0, slot, tile], -1)
            line = jnp.where(lane_block == listed, 1.0, line)
        lines.append(line)
    lines = jnp.concatenate(lines, axis=0).astype(BF)
    for p in (p0, p1):
        p[2 * cols :, :] = lines
    for copy in copies:
        copy.wait()


def correlate(bands, nears, left_zero, corr):
    is_left, is_right, _, _, _ = place()
    cols, channels = left_zero.shape
    ndisp = corr.shape[2]
    group_of = iota((G, channels), 1) // (channels // G)
    gmask = jnp.where(group_of == iota((G, channels), 0), (channels // G) ** -0.5, 0.0).astype(F32)
    lane = iota((G, ndisp), 1)

    def spread(lines):
        lines = lines.astype(F32)
        return jnp.concatenate(
            [(lines[i : i + 1, :] * gmask).astype(BF) for i in range(lines.shape[0])], axis=0
        )

    for c, (xs, xn) in enumerate(zip(bands, nears)):

        def put(xx, value, c=c):
            corr[xx, c * G : c * G + G, :] = value.astype(BF)

        right = slice(cols, 2 * cols)
        near = xn[right, :]
        left_zero[...] = jnp.where(is_left, jnp.zeros_like(near), near)
        masks = xs[2 * cols : 2 * cols + 16, :].astype(F32)
        for k in range(cols // 16):
            x0 = k * 16
            a = spread(xs[x0 : x0 + 16, :])
            hi = lax.dot_general(a, xs[right, :], NT, preferred_element_type=F32)
            lo = lax.dot_general(a, left_zero[...], NT, preferred_element_type=F32)
            m = masks[k : k + 1]
            for i in range(16):
                x = x0 + i
                s = jnp.where(lane <= x, hi[i * G : i * G + G], lo[i * G : i * G + G])
                if x < ndisp - 1:
                    s = pltpu.roll(s, ndisp - 1 - x, 1)
                put(x + 2, s * m)

        mask_n = xn[2 * cols : 2 * cols + 16, :].astype(F32)
        tail = xn[cols - 16 : cols, :].astype(F32)[14:16]
        head = xn[0:16, :].astype(F32)[0:2]
        a = spread(jnp.concatenate([tail, head], axis=0))
        p_n = lax.dot_general(a, xn[right, :], NT, preferred_element_type=F32)
        p_o = lax.dot_general(a, xs[right, :], NT, preferred_element_type=F32)
        m_l = jnp.where(is_left, 0.0, mask_n[15:16])
        m_r = jnp.where(is_right, 0.0, mask_n[0:1])
        s = jnp.where(lane <= ndisp - 2, p_n[0:G], 0.0)
        put(0, pltpu.roll(s, 1, 1) * m_l)
        put(1, p_n[G : 2 * G] * m_l)
        s = jnp.where(lane <= 0, p_n[2 * G : 3 * G], p_o[2 * G : 3 * G])
        put(cols + 2, pltpu.roll(s, ndisp - 1, 1) * m_r)
        s = jnp.where(lane <= 1, p_n[3 * G : 4 * G], p_o[3 * G : 4 * G])
        put(cols + 3, pltpu.roll(s, ndisp - 2, 1) * m_r)


def first_conv(w_own, w_other, own, other, hidden):
    ndisp = own.shape[2]

    def step(s, carry):
        span = pl.ds(s * STEP1, STEP1 + 2)
        depth = (STEP1 + 2) * PAIR
        h = jnp.dot(w_own, own[span].reshape(depth, ndisp), preferred_element_type=F32)
        h += jnp.dot(w_other, other[span].reshape(depth, ndisp), preferred_element_type=F32)
        h = jnp.maximum(h, 0.0).astype(BF)
        hidden[pl.ds(s * STEP1, STEP1)] = h.reshape(STEP1, PAIR, ndisp)
        return carry

    lax.fori_loop(0, hidden.shape[0] // STEP1, step, 0, unroll=8)


def clear_rim(ref, outside, cols):
    is_left, is_right, _, _, _ = place()
    ndisp = ref.shape[2]
    for which in (0, 1):
        @pl.when(outside[which])
        def _():
            def clear(i, carry):
                ref[i, which * G : which * G + G, :] = jnp.zeros((G, ndisp), BF)
                return carry

            lax.fori_loop(0, cols + 2, clear, 0, unroll=8)

    for flag, col in ((is_left, 0), (is_right, cols + 1)):
        @pl.when(flag)
        def _():
            ref[col] = jnp.zeros((PAIR, ndisp), BF)


def tap_row(weights, width):
    pieces = []
    for j in range(3):
        for i in range(3):
            pieces.append(weights[i, j].astype(F32))
        pieces.append(jnp.zeros((G, G), F32))
    pieces.append(jnp.zeros((G, width - 12 * G), F32))
    return jnp.concatenate(pieces, axis=1)


def moved(line, by):
    return (pltpu.roll(line, by, 1) if by else line).astype(BF)


def permuted_columns(matrix, source):
    order = jnp.where(iota(source.shape, 0) == source, 1.0, 0.0).astype(BF)
    return jnp.dot(matrix, order, preferred_element_type=F32).astype(BF)


def weights_kernel(s1, s2, taps, w1, w2, tm):
    ndisp = tm.shape[1]
    depth = (STEP1 + 2) * 4 * G
    line = tap_row(s1, depth)
    plain = [moved(line, (xo * 4 + yo) * G) for xo in range(STEP1) for yo in range(2)]
    c = iota((depth, depth), 1)
    half = depth // 2
    source = ((c % half) // PAIR) * (2 * PAIR) + (c // half) * PAIR + c % PAIR
    sorted_cols = permuted_columns(jnp.concatenate(plain, axis=0), source)
    w1[0] = sorted_cols[:, :half]
    w1[1] = sorted_cols[:, half:]

    line = tap_row(s2, w2.shape[2])
    plain = [moved(line, (xo * 4 + yo) * G) for yo in range(2) for xo in range(STEP2)]
    size = 2 * STEP2 * G
    r = iota((size, size), 0)
    half = STEP2 * G
    source = (r // half) * half + (r % STEP2) * G + (r // STEP2) % G
    order = jnp.where(iota((size, size), 1) == source, 1.0, 0.0).astype(BF)
    plain = jnp.concatenate(plain, axis=0)
    plain = jnp.dot(order, plain, preferred_element_type=F32).astype(BF)
    w2[0] = plain
    c = iota((w2.shape[2], w2.shape[2]), 1)
    w2[1] = permuted_columns(plain, c + PAIR - 2 * PAIR * ((c // PAIR) % 2))

    k = iota((TAPS, ndisp), 0)
    at = iota((TAPS, ndisp), 1)
    spot = TAPS // 2 - k
    spot = jnp.where(spot < 0, spot + ndisp, spot)
    spot = jnp.where(at == spot, 1.0, 0.0).astype(BF)
    lines = jnp.dot(taps[...], spot, preferred_element_type=F32)
    r = iota((ndisp, ndisp), 0)
    c = iota((ndisp, ndisp), 1)
    flip = jnp.where(r + c == ndisp - 1, 1.0, 0.0).astype(BF)
    inside = jnp.abs(r - c) <= TAPS // 2
    for g in range(G):
        line = jnp.broadcast_to(lines[g : g + 1, :], (ndisp, ndisp))
        line = pltpu.roll(line, 0, 1, stride=1, stride_axis=0)
        line = jnp.where(inside, line, 0.0).astype(BF)
        tm[g * ndisp : (g + 1) * ndisp, :] = jnp.dot(
            flip, line, preferred_element_type=F32
        ).astype(BF)


def own_kernel(p0, p1, n0, n1, corr, left_zero):
    correlate((p0, p1), (n0, n1), left_zero, corr)


def partner_kernel(p0, p1, n0, n1, own, w1, hidden, left_zero, corr):
    _, _, first, last, odd = place()
    correlate((p0, p1), (n0, n1), left_zero, corr)
    first_conv(w1[odd], w1[1 - odd], own, corr, hidden)
    clear_rim(hidden, ((odd == 1) & first, (odd == 0) & last), left_zero.shape[0])


def last_kernel(
    p0, p1, n0, n1, own, partner, w1, w2, tm, out_ref, left_zero, corr, hidden, second
):
    _, _, first, last, odd = place()
    cols = left_zero.shape[0]
    ndisp = tm.shape[1]
    correlate((p0, p1), (n0, n1), left_zero, corr)
    first_conv(w1[1 - odd], w1[odd], own, corr, hidden)
    clear_rim(hidden, ((odd == 0) & first, (odd == 1) & last), cols)
    weights = w2[odd]

    def next_hidden(u, carry):
        halves = []
        for v in range(2):
            span = pl.ds((2 * u + v) * STEP2, STEP2 + 2)
            data = jnp.concatenate([hidden[span], partner[span]], axis=1)
            data = data.reshape((STEP2 + 2) * 2 * PAIR, ndisp)
            h = jnp.dot(weights, data, preferred_element_type=F32)
            halves.append(jnp.maximum(h, 0.0))
        for y in range(2):
            for o in range(G):
                r = (y * G + o) * STEP2
                both = jnp.concatenate([h[r : r + STEP2] for h in halves], axis=0)
                second[y, pl.ds(pl.multiple_of(u * 16, 16), 16), o * ndisp : (o + 1) * ndisp] = (
                    both.astype(BF)
                )
        return carry

    lax.fori_loop(0, cols // 16, next_hidden, 0, unroll=4)

    for y in range(2):
        out_ref[y] = jnp.dot(second[y], tm[...], preferred_element_type=F32)


def body(
    left_feat, right_feat, block_list, block_count, spatial_first, spatial_second, disparity_weight
):
    row_count, cols, channels = left_feat.shape
    ndisp = NBLK * DB
    bands = lax.axis_size("rows")
    row = lax.axis_index("rows")
    packed = jax.ShapeDtypeStruct((2 * cols + 16, channels), BF)
    chunks = pl.pallas_call(
        pack_kernel,
        out_shape=[packed, packed],
        in_specs=[HBM, HBM, SMEM, SMEM],
        out_specs=[VMEM, VMEM],
        scratch_shapes=[pltpu.SemaphoreType.DMA((4,))],
        cost_estimate=cost(1),
    )(left_feat, right_feat, block_list.transpose(0, 2, 1), block_count)

    partners = [(i, i ^ 1) for i in range(bands) if i ^ 1 < bands]
    onward = [(i, i + 2 - 4 * (i % 2)) for i in range(bands)]
    onward = [(i, j) for i, j in onward if 0 <= j < bands]
    across = [(0, 1), (1, 0)]

    def cross(x):
        return lax.ppermute(x, "cols", across)

    own_n = [cross(x) for x in chunks]
    by_partner = [lax.ppermute(x, "rows", partners) for x in chunks]
    steps1 = -(-(cols + 2) // STEP1)
    depth1 = (STEP1 + 2) * PAIR
    depth2 = (STEP2 + 2) * 2 * PAIR
    volume = (steps1 * STEP1 + 2, PAIR, ndisp)
    pair = (steps1 * STEP1, PAIR, ndisp)
    left_zero = pltpu.VMEM((cols, channels), BF)

    w1, w2, tm = pl.pallas_call(
        weights_kernel,
        out_shape=[
            jax.ShapeDtypeStruct((2, STEP1 * PAIR, depth1), BF),
            jax.ShapeDtypeStruct((2, STEP2 * PAIR, depth2), BF),
            jax.ShapeDtypeStruct((G * ndisp, ndisp), BF),
        ],
        in_specs=[VMEM] * 3,
        out_specs=[VMEM] * 3,
        compiler_params=LIMIT,
        cost_estimate=cost(4),
    )(spatial_first, spatial_second, disparity_weight.T)

    by_partner[0], w1 = lax.optimization_barrier((by_partner[0], w1))
    by_partner[0], own_n[0] = lax.optimization_barrier((by_partner[0], own_n[0]))
    own = pl.pallas_call(
        own_kernel,
        out_shape=jax.ShapeDtypeStruct(volume, BF),
        in_specs=[VMEM] * 4,
        out_specs=VMEM,
        scratch_shapes=[left_zero],
        compiler_params=LIMIT,
        cost_estimate=cost(4),
    )(*chunks, *own_n)

    def onward_row(c, x):
        if bands % 2:
            x = jnp.where(row == bands - 1, chunks[c], x)
        return lax.ppermute(x, "rows", onward)

    if bands % 2:
        onward.append((bands - 1, bands - 2))
    by_far = [onward_row(0, by_partner[0])]
    by_far[0], own = lax.optimization_barrier((by_far[0], own))
    by_far[0], by_partner[1] = lax.optimization_barrier((by_far[0], by_partner[1]))
    by_far.append(onward_row(1, by_partner[1]))
    by_partner_n = [cross(x) for x in by_partner]
    hidden = pl.pallas_call(
        partner_kernel,
        out_shape=jax.ShapeDtypeStruct(pair, BF),
        in_specs=[VMEM] * 6,
        out_specs=VMEM,
        scratch_shapes=[left_zero, pltpu.VMEM(volume, BF)],
        compiler_params=LIMIT,
        cost_estimate=cost(8),
    )(*by_partner, *by_partner_n, own, w1)

    by_far[1], hidden = lax.optimization_barrier((by_far[1], hidden))
    by_far_n = [cross(x) for x in by_far]
    return pl.pallas_call(
        last_kernel,
        out_shape=jax.ShapeDtypeStruct((row_count, cols, ndisp), F32),
        in_specs=[VMEM] * 9,
        out_specs=VMEM,
        scratch_shapes=[
            left_zero,
            pltpu.VMEM(volume, BF),
            pltpu.VMEM(pair, BF),
            pltpu.VMEM((2, cols, G * ndisp), BF),
        ],
        compiler_params=LIMIT,
        cost_estimate=cost(12),
    )(*by_far, *by_far_n, own, hidden, w1, w2, tm)


def solution(mesh):
    in_specs = (
        P(("pairs", "rows"), "cols", None),
        P(("pairs", "rows"), "cols", None),
        P(("pairs", "rows"), "cols", None),
        P(("pairs", "rows"), "cols"),
        P(),
        P(),
        P(),
    )
    out_specs = P(("pairs", "rows"), "cols", None)
    return jax.shard_map(body, mesh=mesh, in_specs=in_specs, out_specs=out_specs, check_vma=False)
```

```python
import jax
import jax.numpy as jnp
from jax import lax
from jax.experimental import pallas as pl
from jax.experimental.pallas import tpu as pltpu
from jax.sharding import PartitionSpec as P

G = 16
DB = 128
NBLK = 2
TILE = 64
TAPS = 17
STEP1 = 6
STEP2 = 8
PAIR = 2 * G
BF = jnp.bfloat16
F32 = jnp.float32
NT = (((1,), (1,)), ((), ()))
VMEM = pl.BlockSpec(memory_space=pltpu.VMEM)
SMEM = pl.BlockSpec(memory_space=pltpu.SMEM)
HBM = pl.BlockSpec(memory_space=pl.ANY)
LIMIT = pltpu.CompilerParams(vmem_limit_bytes=36 * 1024 * 1024)


def cost(us):
    return pl.CostEstimate(flops=us * 10**9, bytes_accessed=us * 10**6, transcendentals=0)


def iota(shape, dim):
    return lax.broadcasted_iota(jnp.int32, shape, dim)


def place():
    row, col = lax.axis_index("rows"), lax.axis_index("cols")
    rows, cols = lax.axis_size("rows"), lax.axis_size("cols")
    return col == 0, col == cols - 1, row == 0, row == rows - 1, row % 2


def pack_kernel(left, right, block_list, block_count, p0, p1, sems):
    cols = left.shape[1]
    copies = []
    for c, p in enumerate((p0, p1)):
        for i, src in enumerate((left, right)):
            dst = p.at[pl.ds(i * cols, cols), :]
            copies.append(pltpu.make_async_copy(src.at[c], dst, sems.at[2 * c + i]))
            copies[-1].start()
    ndisp = p0.shape[1]
    lane_block = (ndisp - 1 - iota((TILE // 16, ndisp), 1)) // DB
    lines = []
    for tile in range(cols // TILE):
        line = jnp.zeros(lane_block.shape, F32)
        for slot in range(block_list.shape[1]):
            listed = jnp.where(slot < block_count[0, tile], block_list[0, slot, tile], -1)
            line = jnp.where(lane_block == listed, 1.0, line)
        lines.append(line)
    lines = jnp.concatenate(lines, axis=0).astype(BF)
    for p in (p0, p1):
        p[2 * cols :, :] = lines
    for copy in copies:
        copy.wait()


def correlate(rows, left_zero):
    is_left, is_right, _, _, _ = place()
    cols, channels = left_zero.shape
    ndisp = NBLK * DB
    group_of = iota((G, channels), 1) // (channels // G)
    gmask = jnp.where(group_of == iota((G, channels), 0), (channels // G) ** -0.5, 0.0).astype(F32)
    lane = iota((G, ndisp), 1)

    def spread(lines):
        lines = lines.astype(F32)
        return jnp.concatenate(
            [(lines[i : i + 1, :] * gmask).astype(BF) for i in range(lines.shape[0])], axis=0
        )

    for xs, xn, corr in rows:

        def put(xx, value, corr=corr):
            corr[xx] = value.astype(BF)

        right = slice(cols, 2 * cols)
        near = xn[right, :]
        left_zero[...] = jnp.where(is_left, jnp.zeros_like(near), near)
        masks = xs[2 * cols : 2 * cols + 16, :].astype(F32)
        for k in range(cols // 16):
            x0 = k * 16
            a = spread(xs[x0 : x0 + 16, :])
            hi = lax.dot_general(a, xs[right, :], NT, preferred_element_type=F32)
            lo = lax.dot_general(a, left_zero[...], NT, preferred_element_type=F32)
            m = masks[k : k + 1]
            for i in range(16):
                x = x0 + i
                s = jnp.where(lane <= x, hi[i * G : i * G + G], lo[i * G : i * G + G])
                if x < ndisp - 1:
                    s = pltpu.roll(s, ndisp - 1 - x, 1)
                put(x + 2, s * m)

        mask_n = xn[2 * cols : 2 * cols + 16, :].astype(F32)
        tail = xn[cols - 16 : cols, :].astype(F32)[14:16]
        head = xn[0:16, :].astype(F32)[0:2]
        a = spread(jnp.concatenate([tail, head], axis=0))
        p_n = lax.dot_general(a, xn[right, :], NT, preferred_element_type=F32)
        p_o = lax.dot_general(a, xs[right, :], NT, preferred_element_type=F32)
        m_l = jnp.where(is_left, 0.0, mask_n[15:16])
        m_r = jnp.where(is_right, 0.0, mask_n[0:1])
        s = jnp.where(lane <= ndisp - 2, p_n[0:G], 0.0)
        put(0, pltpu.roll(s, 1, 1) * m_l)
        put(1, p_n[G : 2 * G] * m_l)
        s = jnp.where(lane <= 0, p_n[2 * G : 3 * G], p_o[2 * G : 3 * G])
        put(cols + 2, pltpu.roll(s, ndisp - 1, 1) * m_r)
        s = jnp.where(lane <= 1, p_n[3 * G : 4 * G], p_o[3 * G : 4 * G])
        put(cols + 3, pltpu.roll(s, ndisp - 2, 1) * m_r)


def row_block(refs, span):
    data = jnp.concatenate([ref[span] for ref in refs], axis=1)
    return data.reshape(data.shape[0] * data.shape[1], data.shape[2])


def first_conv(w_own, w_other, own, other, hidden):
    def step(s, carry):
        span = pl.ds(s * STEP1, STEP1 + 2)
        h = jnp.dot(w_own, row_block(own, span), preferred_element_type=F32)
        h += jnp.dot(w_other, row_block(other, span), preferred_element_type=F32)
        h = jnp.maximum(h, 0.0).astype(BF)
        hidden[pl.ds(s * STEP1, STEP1)] = h.reshape(STEP1, PAIR, h.shape[1])
        return carry

    lax.fori_loop(0, hidden.shape[0] // STEP1, step, 0, unroll=True)


def clear_rim(ref, outside, cols):
    is_left, is_right, _, _, _ = place()
    ndisp = ref.shape[2]
    for which in (0, 1):
        @pl.when(outside[which])
        def _():
            def clear(i, carry):
                ref[i, which * G : which * G + G, :] = jnp.zeros((G, ndisp), BF)
                return carry

            lax.fori_loop(0, cols + 2, clear, 0, unroll=8)

    for flag, col in ((is_left, 0), (is_right, cols + 1)):
        @pl.when(flag)
        def _():
            ref[col] = jnp.zeros((PAIR, ndisp), BF)


def tap_row(weights, order, width):
    pieces = []
    for j in range(3):
        for i in order:
            pieces.append(jnp.zeros((G, G), F32) if i is None else weights[i, j].astype(F32))
    pieces.append(jnp.zeros((G, width - 3 * len(order) * G), F32))
    return jnp.concatenate(pieces, axis=1)


def moved(line, by):
    return (pltpu.roll(line, by, 1) if by else line).astype(BF)


def permuted_columns(matrix, source):
    order = jnp.where(iota(source.shape, 0) == source, 1.0, 0.0).astype(BF)
    return jnp.dot(matrix, order, preferred_element_type=F32).astype(BF)


def weights_kernel(s1, s2, taps, w1, w2, tm):
    ndisp = tm.shape[1]
    depth = (STEP1 + 2) * 4 * G
    line = tap_row(s1, (0, 1, 2, None), depth)
    plain = [moved(line, (xo * 4 + yo) * G) for xo in range(STEP1) for yo in range(2)]
    c = iota((depth, depth), 1)
    half = depth // 2
    source = ((c % half) // PAIR) * (2 * PAIR) + (c // half) * PAIR + c % PAIR
    sorted_cols = permuted_columns(jnp.concatenate(plain, axis=0), source)
    w1[0] = sorted_cols[:, :half]
    w1[1] = sorted_cols[:, half:]

    size = STEP2 * G
    r = iota((size, size), 0)
    source = (r % STEP2) * G + r // STEP2
    order = jnp.where(iota((size, size), 1) == source, 1.0, 0.0).astype(BF)
    for v, taps_order in enumerate(((0, 1, 2), (1, 2, 0), (2, 0, 1))):
        line = tap_row(s2, taps_order, w2.shape[2])
        plain = jnp.concatenate([moved(line, xo * 3 * G) for xo in range(STEP2)], axis=0)
        w2[v] = jnp.dot(order, plain, preferred_element_type=F32).astype(BF)

    k = iota((TAPS, ndisp), 0)
    at = iota((TAPS, ndisp), 1)
    spot = TAPS // 2 - k
    spot = jnp.where(spot < 0, spot + ndisp, spot)
    spot = jnp.where(at == spot, 1.0, 0.0).astype(BF)
    lines = jnp.dot(taps[...], spot, preferred_element_type=F32)
    r = iota((ndisp, ndisp), 0)
    c = iota((ndisp, ndisp), 1)
    flip = jnp.where(r + c == ndisp - 1, 1.0, 0.0).astype(BF)
    inside = jnp.abs(r - c) <= TAPS // 2
    for g in range(G):
        line = jnp.broadcast_to(lines[g : g + 1, :], (ndisp, ndisp))
        line = pltpu.roll(line, 0, 1, stride=1, stride_axis=0)
        line = jnp.where(inside, line, 0.0).astype(BF)
        tm[g * ndisp : (g + 1) * ndisp, :] = jnp.dot(
            flip, line, preferred_element_type=F32
        ).astype(BF)


def own_kernel(own0, own1, own0_n, own1_n, o0, o1, left_zero):
    correlate(((own0, own0_n, o0), (own1, own1_n, o1)), left_zero)


def partner_kernel(par0, par1, par0_n, par1_n, o0, o1, w1, hidden, left_zero, p0, p1):
    _, _, first, last, odd = place()
    correlate(((par0, par0_n, p0), (par1, par1_n, p1)), left_zero)
    first_conv(w1[odd], w1[1 - odd], (o0, o1), (p0, p1), hidden)
    clear_rim(hidden, ((odd == 1) & first, (odd == 0) & last), left_zero.shape[0])


def row_kernel(xs, xn, corr, left_zero):
    correlate(((xs, xn, corr),), left_zero)


def last_kernel(
    far1, far1_n, f0, o0, o1, partner, w1, w2, tm, out_ref, left_zero, f1, hidden, second
):
    _, _, first, last, odd = place()
    cols = left_zero.shape[0]
    ndisp = tm.shape[1]
    correlate(((far1, far1_n, f1),), left_zero)
    first_conv(w1[1 - odd], w1[odd], (o0, o1), (f0, f1), hidden)
    clear_rim(hidden, ((odd == 0) & first, (odd == 1) & last), cols)
    one = pl.ds(pl.multiple_of(odd * G, G), G)
    other = pl.ds(pl.multiple_of((1 - odd) * G, G), G)
    outputs = ((odd, w2[odd]), (1 - odd, w2[2 * odd]))

    def next_hidden(u, carry):
        halves = ([], [])
        for v in range(2):
            span = pl.ds((2 * u + v) * STEP2, STEP2 + 2)
            blocks = ((hidden[span], partner[span, one, :]), (hidden[span, other, :], partner[span]))
            for half, block, (_, weights) in zip(halves, blocks, outputs):
                data = jnp.concatenate(block, axis=1).reshape((STEP2 + 2) * 3 * G, ndisp)
                h = jnp.dot(weights, data, preferred_element_type=F32)
                half.append(jnp.maximum(h, 0.0))
        for half, (y, _) in zip(halves, outputs):
            for o in range(G):
                r = o * STEP2
                both = jnp.concatenate([h[r : r + STEP2] for h in half], axis=0)
                second[y, pl.ds(pl.multiple_of(u * 16, 16), 16), o * ndisp : (o + 1) * ndisp] = (
                    both.astype(BF)
                )
        return carry

    lax.fori_loop(0, cols // 16, next_hidden, 0, unroll=True)

    for y in range(2):
        out_ref[y] = jnp.dot(second[y], tm[...], preferred_element_type=F32)


def body(
    left_feat, right_feat, block_list, block_count, spatial_first, spatial_second, disparity_weight
):
    row_count, cols, channels = left_feat.shape
    ndisp = NBLK * DB
    bands = lax.axis_size("rows")
    row = lax.axis_index("rows")
    packed = jax.ShapeDtypeStruct((2 * cols + 16, channels), BF)
    chunks = pl.pallas_call(
        pack_kernel,
        out_shape=[packed, packed],
        in_specs=[HBM, HBM, SMEM, SMEM],
        out_specs=[VMEM, VMEM],
        scratch_shapes=[pltpu.SemaphoreType.DMA((4,))],
        cost_estimate=cost(1),
    )(left_feat, right_feat, block_list.transpose(0, 2, 1), block_count)

    partners = [(i, i ^ 1) for i in range(bands) if i ^ 1 < bands]
    onward = [(i, i + 2 - 4 * (i % 2)) for i in range(bands)]
    onward = [(i, j) for i, j in onward if 0 <= j < bands]
    across = [(0, 1), (1, 0)]

    def cross(x):
        return lax.ppermute(x, "cols", across)

    par0, par1 = [lax.ppermute(x, "rows", partners) for x in chunks]
    own_n = [cross(x) for x in chunks]
    steps1 = -(-(cols + 2) // STEP1)
    depth1 = (STEP1 + 2) * PAIR
    depth2 = (STEP2 + 2) * 3 * G
    volume = (steps1 * STEP1 + 2, G, ndisp)
    volume_out = jax.ShapeDtypeStruct(volume, BF)
    pair = (steps1 * STEP1, PAIR, ndisp)
    left_zero = pltpu.VMEM((cols, channels), BF)

    w1, w2, tm = pl.pallas_call(
        weights_kernel,
        out_shape=[
            jax.ShapeDtypeStruct((2, STEP1 * PAIR, depth1), BF),
            jax.ShapeDtypeStruct((3, STEP2 * G, depth2), BF),
            jax.ShapeDtypeStruct((G * ndisp, ndisp), BF),
        ],
        in_specs=[VMEM] * 3,
        out_specs=[VMEM] * 3,
        compiler_params=LIMIT,
        cost_estimate=cost(4),
    )(spatial_first, spatial_second, disparity_weight.T)

    par0, w1 = lax.optimization_barrier((par0, w1))
    if bands % 2:
        onward.append((bands - 1, bands - 2))

    def send_on(chunk, x):
        if bands % 2:
            x = jnp.where(row == bands - 1, chunk, x)
        return lax.ppermute(x, "rows", onward)

    far0 = send_on(chunks[0], par0)
    par0_n = cross(par0)

    par0, own_n[0] = lax.optimization_barrier((par0, own_n[0]))
    o0, o1 = pl.pallas_call(
        own_kernel,
        out_shape=[volume_out] * 2,
        in_specs=[VMEM] * 4,
        out_specs=[VMEM] * 2,
        scratch_shapes=[left_zero],
        compiler_params=LIMIT,
        cost_estimate=cost(4),
    )(*chunks, *own_n)
    far0, o0 = lax.optimization_barrier((far0, o0))
    par1, o1 = lax.optimization_barrier((par1, o1))
    far1 = send_on(chunks[1], par1)
    par1_n = cross(par1)
    par1_n, far0 = lax.optimization_barrier((par1_n, far0))

    hidden = pl.pallas_call(
        partner_kernel,
        out_shape=jax.ShapeDtypeStruct(pair, BF),
        in_specs=[VMEM] * 7,
        out_specs=VMEM,
        scratch_shapes=[left_zero, pltpu.VMEM(volume, BF), pltpu.VMEM(volume, BF)],
        compiler_params=LIMIT,
        cost_estimate=cost(8),
    )(par0, par1, par0_n, par1_n, o0, o1, w1)
    far0_n = cross(far0)
    far1, hidden = lax.optimization_barrier((far1, hidden))
    f0 = pl.pallas_call(
        row_kernel,
        out_shape=volume_out,
        in_specs=[VMEM] * 2,
        out_specs=VMEM,
        scratch_shapes=[left_zero],
        compiler_params=LIMIT,
        cost_estimate=cost(1),
    )(far0, far0_n)

    return pl.pallas_call(
        last_kernel,
        out_shape=jax.ShapeDtypeStruct((row_count, cols, ndisp), F32),
        in_specs=[VMEM] * 9,
        out_specs=VMEM,
        scratch_shapes=[
            left_zero,
            pltpu.VMEM(volume, BF),
            pltpu.VMEM(pair, BF),
            pltpu.VMEM((2, cols, G * ndisp), BF),
        ],
        compiler_params=LIMIT,
        cost_estimate=cost(12),
    )(far1, cross(far1), f0, o0, o1, hidden, w1, w2, tm)


def solution(mesh):
    in_specs = (
        P(("pairs", "rows"), "cols", None),
        P(("pairs", "rows"), "cols", None),
        P(("pairs", "rows"), "cols", None),
        P(("pairs", "rows"), "cols"),
        P(),
        P(),
        P(),
    )
    out_specs = P(("pairs", "rows"), "cols", None)
    return jax.shard_map(body, mesh=mesh, in_specs=in_specs, out_specs=out_specs, check_vma=False)
```

```python
import jax
import jax.numpy as jnp
from jax import lax
from jax.experimental import pallas as pl
from jax.experimental.pallas import tpu as pltpu
from jax.sharding import PartitionSpec as P

G = 16
DB = 128
NBLK = 2
TILE = 64
TAPS = 17
STEP1 = 6
STEP2 = 8
PAIR = 2 * G
BF = jnp.bfloat16
F32 = jnp.float32
NT = (((1,), (1,)), ((), ()))
VMEM = pl.BlockSpec(memory_space=pltpu.VMEM)
SMEM = pl.BlockSpec(memory_space=pltpu.SMEM)
HBM = pl.BlockSpec(memory_space=pl.ANY)
LIMIT = pltpu.CompilerParams(vmem_limit_bytes=36 * 1024 * 1024)


def cost(us):
    return pl.CostEstimate(flops=us * 10**9, bytes_accessed=us * 10**6, transcendentals=0)


def iota(shape, dim):
    return lax.broadcasted_iota(jnp.int32, shape, dim)


def place():
    row, col = lax.axis_index("rows"), lax.axis_index("cols")
    rows, cols = lax.axis_size("rows"), lax.axis_size("cols")
    return col == 0, col == cols - 1, row == 0, row == rows - 1, row % 2


def pack_kernel(left, right, block_list, block_count, p0, p1, sems):
    cols = left.shape[1]
    copies = []
    for c, p in enumerate((p0, p1)):
        for i, src in enumerate((left, right)):
            dst = p.at[pl.ds(i * cols, cols), :]
            copies.append(pltpu.make_async_copy(src.at[c], dst, sems.at[2 * c + i]))
            copies[-1].start()
    ndisp = p0.shape[1]
    lane_block = (ndisp - 1 - iota((TILE // 16, ndisp), 1)) // DB
    lines = []
    for tile in range(cols // TILE):
        line = jnp.zeros(lane_block.shape, F32)
        for slot in range(block_list.shape[1]):
            listed = jnp.where(slot < block_count[0, tile], block_list[0, slot, tile], -1)
            line = jnp.where(lane_block == listed, 1.0, line)
        lines.append(line)
    lines = jnp.concatenate(lines, axis=0).astype(BF)
    for p in (p0, p1):
        p[2 * cols :, :] = lines
    for copy in copies:
        copy.wait()


def correlate(rows, left_zero):
    is_left, is_right, _, _, _ = place()
    cols, channels = left_zero.shape
    ndisp = NBLK * DB
    group_of = iota((G, channels), 1) // (channels // G)
    gmask = jnp.where(group_of == iota((G, channels), 0), (channels // G) ** -0.5, 0.0).astype(F32)
    lane = iota((G, ndisp), 1)

    def spread(lines):
        lines = lines.astype(F32)
        return jnp.concatenate(
            [(lines[i : i + 1, :] * gmask).astype(BF) for i in range(lines.shape[0])], axis=0
        )

    for xs, xn, corr in rows:

        def put(xx, value, corr=corr):
            corr[xx] = value.astype(BF)

        right = slice(cols, 2 * cols)
        near = xn[right, :]
        left_zero[...] = jnp.where(is_left, jnp.zeros_like(near), near)
        masks = xs[2 * cols : 2 * cols + 16, :].astype(F32)
        for k in range(cols // 16):
            x0 = k * 16
            a = spread(xs[x0 : x0 + 16, :])
            hi = lax.dot_general(a, xs[right, :], NT, preferred_element_type=F32)
            lo = lax.dot_general(a, left_zero[...], NT, preferred_element_type=F32)
            m = masks[k : k + 1]
            for i in range(16):
                x = x0 + i
                s = jnp.where(lane <= x, hi[i * G : i * G + G], lo[i * G : i * G + G])
                if x < ndisp - 1:
                    s = pltpu.roll(s, ndisp - 1 - x, 1)
                put(x + 2, s * m)

        mask_n = xn[2 * cols : 2 * cols + 16, :].astype(F32)
        tail = xn[cols - 16 : cols, :].astype(F32)[14:16]
        head = xn[0:16, :].astype(F32)[0:2]
        a = spread(jnp.concatenate([tail, head], axis=0))
        p_n = lax.dot_general(a, xn[right, :], NT, preferred_element_type=F32)
        p_o = lax.dot_general(a, xs[right, :], NT, preferred_element_type=F32)
        m_l = jnp.where(is_left, 0.0, mask_n[15:16])
        m_r = jnp.where(is_right, 0.0, mask_n[0:1])
        s = jnp.where(lane <= ndisp - 2, p_n[0:G], 0.0)
        put(0, pltpu.roll(s, 1, 1) * m_l)
        put(1, p_n[G : 2 * G] * m_l)
        s = jnp.where(lane <= 0, p_n[2 * G : 3 * G], p_o[2 * G : 3 * G])
        put(cols + 2, pltpu.roll(s, ndisp - 1, 1) * m_r)
        s = jnp.where(lane <= 1, p_n[3 * G : 4 * G], p_o[3 * G : 4 * G])
        put(cols + 3, pltpu.roll(s, ndisp - 2, 1) * m_r)


def row_block(refs, span):
    data = jnp.concatenate([ref[span] for ref in refs], axis=1)
    return data.reshape(data.shape[0] * data.shape[1], data.shape[2])


def first_conv(w_own, w_other, own, other, hidden):
    def step(s, carry):
        span = pl.ds(s * STEP1, STEP1 + 2)
        h = jnp.dot(w_own, row_block(own, span), preferred_element_type=F32)
        h += jnp.dot(w_other, row_block(other, span), preferred_element_type=F32)
        h = jnp.maximum(h, 0.0).astype(BF)
        hidden[pl.ds(s * STEP1, STEP1)] = h.reshape(STEP1, PAIR, h.shape[1])
        return carry

    lax.fori_loop(0, hidden.shape[0] // STEP1, step, 0, unroll=True)


def clear_rim(ref, outside, cols):
    is_left, is_right, _, _, _ = place()
    ndisp = ref.shape[2]
    for which in (0, 1):
        @pl.when(outside[which])
        def _():
            def clear(i, carry):
                ref[i, which * G : which * G + G, :] = jnp.zeros((G, ndisp), BF)
                return carry

            lax.fori_loop(0, cols + 2, clear, 0, unroll=8)

    for flag, col in ((is_left, 0), (is_right, cols + 1)):
        @pl.when(flag)
        def _():
            ref[col] = jnp.zeros((PAIR, ndisp), BF)


def tap_row(weights, order, width):
    pieces = []
    for j in range(3):
        for i in order:
            pieces.append(jnp.zeros((G, G), F32) if i is None else weights[i, j].astype(F32))
    pieces.append(jnp.zeros((G, width - 3 * len(order) * G), F32))
    return jnp.concatenate(pieces, axis=1)


def moved(line, by):
    return (pltpu.roll(line, by, 1) if by else line).astype(BF)


def permuted_columns(matrix, source):
    order = jnp.where(iota(source.shape, 0) == source, 1.0, 0.0).astype(BF)
    return jnp.dot(matrix, order, preferred_element_type=F32).astype(BF)


def weights_kernel(s1, s2, taps, w1, w2, tm):
    ndisp = tm.shape[1]
    depth = (STEP1 + 2) * 4 * G
    line = tap_row(s1, (0, 1, 2, None), depth)
    plain = [moved(line, (xo * 4 + yo) * G) for xo in range(STEP1) for yo in range(2)]
    c = iota((depth, depth), 1)
    half = depth // 2
    source = ((c % half) // PAIR) * (2 * PAIR) + (c // half) * PAIR + c % PAIR
    sorted_cols = permuted_columns(jnp.concatenate(plain, axis=0), source)
    w1[0] = sorted_cols[:, :half]
    w1[1] = sorted_cols[:, half:]

    size = STEP2 * G
    r = iota((size, size), 0)
    source = (r % STEP2) * G + r // STEP2
    order = jnp.where(iota((size, size), 1) == source, 1.0, 0.0).astype(BF)
    for v, taps_order in enumerate(((0, 1, 2), (1, 2, 0), (2, 0, 1))):
        line = tap_row(s2, taps_order, w2.shape[2])
        plain = jnp.concatenate([moved(line, xo * 3 * G) for xo in range(STEP2)], axis=0)
        w2[v] = jnp.dot(order, plain, preferred_element_type=F32).astype(BF)

    k = iota((TAPS, ndisp), 0)
    at = iota((TAPS, ndisp), 1)
    spot = TAPS // 2 - k
    spot = jnp.where(spot < 0, spot + ndisp, spot)
    spot = jnp.where(at == spot, 1.0, 0.0).astype(BF)
    lines = jnp.dot(taps[...], spot, preferred_element_type=F32)
    r = iota((ndisp, ndisp), 0)
    c = iota((ndisp, ndisp), 1)
    flip = jnp.where(r + c == ndisp - 1, 1.0, 0.0).astype(BF)
    inside = jnp.abs(r - c) <= TAPS // 2
    for g in range(G):
        line = jnp.broadcast_to(lines[g : g + 1, :], (ndisp, ndisp))
        line = pltpu.roll(line, 0, 1, stride=1, stride_axis=0)
        line = jnp.where(inside, line, 0.0).astype(BF)
        tm[g * ndisp : (g + 1) * ndisp, :] = jnp.dot(
            flip, line, preferred_element_type=F32
        ).astype(BF)


def own_kernel(own0, own1, own0_n, own1_n, o0, o1, left_zero):
    correlate(((own0, own0_n, o0), (own1, own1_n, o1)), left_zero)


def partner_kernel(par0, par1, par0_n, par1_n, o0, o1, w1, hidden, left_zero, p0, p1):
    _, _, first, last, odd = place()
    correlate(((par0, par0_n, p0), (par1, par1_n, p1)), left_zero)
    first_conv(w1[odd], w1[1 - odd], (o0, o1), (p0, p1), hidden)
    clear_rim(hidden, ((odd == 1) & first, (odd == 0) & last), left_zero.shape[0])


def row_kernel(xs, xn, corr, left_zero):
    correlate(((xs, xn, corr),), left_zero)


def last_kernel(
    far1, far1_n, f0, o0, o1, partner, w1, w2, tm, out_ref, left_zero, f1, hidden, second
):
    _, _, first, last, odd = place()
    cols = left_zero.shape[0]
    ndisp = tm.shape[1]
    correlate(((far1, far1_n, f1),), left_zero)
    first_conv(w1[1 - odd], w1[odd], (o0, o1), (f0, f1), hidden)
    clear_rim(hidden, ((odd == 0) & first, (odd == 1) & last), cols)
    one = pl.ds(pl.multiple_of(odd * G, G), G)
    other = pl.ds(pl.multiple_of((1 - odd) * G, G), G)
    outputs = ((odd, w2[odd]), (1 - odd, w2[2 * odd]))

    def next_hidden(u, carry):
        halves = ([], [])
        for v in range(2):
            span = pl.ds((2 * u + v) * STEP2, STEP2 + 2)
            blocks = ((hidden[span], partner[span, one, :]), (hidden[span, other, :], partner[span]))
            for half, block, (_, weights) in zip(halves, blocks, outputs):
                data = jnp.concatenate(block, axis=1).reshape((STEP2 + 2) * 3 * G, ndisp)
                h = jnp.dot(weights, data, preferred_element_type=F32)
                half.append(jnp.maximum(h, 0.0))
        for half, (y, _) in zip(halves, outputs):
            for o in range(G):
                r = o * STEP2
                both = jnp.concatenate([h[r : r + STEP2] for h in half], axis=0)
                second[y, pl.ds(pl.multiple_of(u * 16, 16), 16), o * ndisp : (o + 1) * ndisp] = (
                    both.astype(BF)
                )
        return carry

    lax.fori_loop(0, cols // 16, next_hidden, 0, unroll=True)

    for y in range(2):
        out_ref[y] = jnp.dot(second[y], tm[...], preferred_element_type=F32)


def body(
    left_feat, right_feat, block_list, block_count, spatial_first, spatial_second, disparity_weight
):
    row_count, cols, channels = left_feat.shape
    ndisp = NBLK * DB
    bands = lax.axis_size("rows")
    row = lax.axis_index("rows")
    packed = jax.ShapeDtypeStruct((2 * cols + 16, channels), BF)
    chunks = pl.pallas_call(
        pack_kernel,
        out_shape=[packed, packed],
        in_specs=[HBM, HBM, SMEM, SMEM],
        out_specs=[VMEM, VMEM],
        scratch_shapes=[pltpu.SemaphoreType.DMA((4,))],
        cost_estimate=cost(1),
    )(left_feat, right_feat, block_list.transpose(0, 2, 1), block_count)

    partners = [(i, i ^ 1) for i in range(bands) if i ^ 1 < bands]
    onward = [(i, i + 2 - 4 * (i % 2)) for i in range(bands)]
    onward = [(i, j) for i, j in onward if 0 <= j < bands]
    across = [(0, 1), (1, 0)]

    def cross(x):
        return lax.ppermute(x, "cols", across)

    par0, par1 = [lax.ppermute(x, "rows", partners) for x in chunks]
    own_n = [cross(x) for x in chunks]
    steps1 = -(-(cols + 2) // STEP1)
    depth1 = (STEP1 + 2) * PAIR
    depth2 = (STEP2 + 2) * 3 * G
    volume = (steps1 * STEP1 + 2, G, ndisp)
    volume_out = jax.ShapeDtypeStruct(volume, BF)
    pair = (steps1 * STEP1, PAIR, ndisp)
    left_zero = pltpu.VMEM((cols, channels), BF)

    w1, w2, tm = pl.pallas_call(
        weights_kernel,
        out_shape=[
            jax.ShapeDtypeStruct((2, STEP1 * PAIR, depth1), BF),
            jax.ShapeDtypeStruct((3, STEP2 * G, depth2), BF),
            jax.ShapeDtypeStruct((G * ndisp, ndisp), BF),
        ],
        in_specs=[VMEM] * 3,
        out_specs=[VMEM] * 3,
        compiler_params=LIMIT,
        cost_estimate=cost(4),
    )(spatial_first, spatial_second, disparity_weight.T)

    o0, o1 = pl.pallas_call(
        own_kernel,
        out_shape=[volume_out] * 2,
        in_specs=[VMEM] * 4,
        out_specs=[VMEM] * 2,
        scratch_shapes=[left_zero],
        compiler_params=LIMIT,
        cost_estimate=cost(4),
    )(*chunks, *own_n)
    par0, w1, o0 = lax.optimization_barrier((par0, w1, o0))
    if bands % 2:
        onward.append((bands - 1, bands - 2))

    def send_on(chunk, x):
        if bands % 2:
            x = jnp.where(row == bands - 1, chunk, x)
        return lax.ppermute(x, "rows", onward)

    far0 = send_on(chunks[0], par0)
    par0_n = cross(par0)

    far1 = send_on(chunks[1], par1)
    par1_n = cross(par1)
    par1_n, far0 = lax.optimization_barrier((par1_n, far0))

    hidden = pl.pallas_call(
        partner_kernel,
        out_shape=jax.ShapeDtypeStruct(pair, BF),
        in_specs=[VMEM] * 7,
        out_specs=VMEM,
        scratch_shapes=[left_zero, pltpu.VMEM(volume, BF), pltpu.VMEM(volume, BF)],
        compiler_params=LIMIT,
        cost_estimate=cost(8),
    )(par0, par1, par0_n, par1_n, o0, o1, w1)
    far0_n = cross(far0)
    far1, hidden = lax.optimization_barrier((far1, hidden))
    f0 = pl.pallas_call(
        row_kernel,
        out_shape=volume_out,
        in_specs=[VMEM] * 2,
        out_specs=VMEM,
        scratch_shapes=[left_zero],
        compiler_params=LIMIT,
        cost_estimate=cost(1),
    )(far0, far0_n)

    return pl.pallas_call(
        last_kernel,
        out_shape=jax.ShapeDtypeStruct((row_count, cols, ndisp), F32),
        in_specs=[VMEM] * 9,
        out_specs=VMEM,
        scratch_shapes=[
            left_zero,
            pltpu.VMEM(volume, BF),
            pltpu.VMEM(pair, BF),
            pltpu.VMEM((2, cols, G * ndisp), BF),
        ],
        compiler_params=LIMIT,
        cost_estimate=cost(12),
    )(far1, cross(far1), f0, o0, o1, hidden, w1, w2, tm)


def solution(mesh):
    in_specs = (
        P(("pairs", "rows"), "cols", None),
        P(("pairs", "rows"), "cols", None),
        P(("pairs", "rows"), "cols", None),
        P(("pairs", "rows"), "cols"),
        P(),
        P(),
        P(),
    )
    out_specs = P(("pairs", "rows"), "cols", None)
    return jax.shard_map(body, mesh=mesh, in_specs=in_specs, out_specs=out_specs, check_vma=False)
```

```python
import functools

import jax
import jax.numpy as jnp
from jax import lax
from jax.experimental import pallas as pl
from jax.experimental.pallas import tpu as pltpu
from jax.sharding import PartitionSpec as P

G = 16
DB = 128
NBLK = 2
TILE = 64
TAPS = 17
STEP1 = 6
STEP2 = 8
PAIR = 2 * G
BF = jnp.bfloat16
F32 = jnp.float32
NT = (((1,), (1,)), ((), ()))
VMEM = pl.BlockSpec(memory_space=pltpu.VMEM)
SMEM = pl.BlockSpec(memory_space=pltpu.SMEM)
HBM = pl.BlockSpec(memory_space=pl.ANY)
LIMIT = pltpu.CompilerParams(vmem_limit_bytes=36 * 1024 * 1024)


def cost(us):
    return pl.CostEstimate(flops=us * 10**9, bytes_accessed=us * 10**6, transcendentals=0)


def iota(shape, dim):
    return lax.broadcasted_iota(jnp.int32, shape, dim)


def place():
    row, col = lax.axis_index("rows"), lax.axis_index("cols")
    rows, cols = lax.axis_size("rows"), lax.axis_size("cols")
    return col == 0, col == cols - 1, row == 0, row == rows - 1, row % 2


def pack_kernel(c, left, right, block_list, block_count, pack, sems):
    cols = left.shape[1]
    copies = []
    for i, src in enumerate((left, right)):
        dst = pack.at[pl.ds(i * cols, cols), :]
        copies.append(pltpu.make_async_copy(src.at[c], dst, sems.at[i]))
        copies[-1].start()
    ndisp = pack.shape[1]
    lane_block = (ndisp - 1 - iota((TILE // 16, ndisp), 1)) // DB
    lines = []
    for tile in range(cols // TILE):
        line = jnp.zeros(lane_block.shape, F32)
        for slot in range(block_list.shape[1]):
            listed = jnp.where(slot < block_count[0, tile], block_list[0, slot, tile], -1)
            line = jnp.where(lane_block == listed, 1.0, line)
        lines.append(line)
    pack[2 * cols :, :] = jnp.concatenate(lines, axis=0).astype(BF)
    for copy in copies:
        copy.wait()


def correlate(rows, left_zero):
    is_left, is_right, _, _, _ = place()
    cols, channels = left_zero.shape
    ndisp = NBLK * DB
    group_of = iota((G, channels), 1) // (channels // G)
    gmask = jnp.where(group_of == iota((G, channels), 0), (channels // G) ** -0.5, 0.0).astype(F32)
    lane = iota((G, ndisp), 1)

    def spread(lines):
        lines = lines.astype(F32)
        return jnp.concatenate(
            [(lines[i : i + 1, :] * gmask).astype(BF) for i in range(lines.shape[0])], axis=0
        )

    for xs, xn, corr in rows:

        def put(xx, value, corr=corr):
            corr[xx] = value.astype(BF)

        right = slice(cols, 2 * cols)
        near = xn[right, :]
        left_zero[...] = jnp.where(is_left, jnp.zeros_like(near), near)
        masks = xs[2 * cols : 2 * cols + 16, :].astype(F32)
        for k in range(cols // 16):
            x0 = k * 16
            a = spread(xs[x0 : x0 + 16, :])
            hi = lax.dot_general(a, xs[right, :], NT, preferred_element_type=F32)
            lo = lax.dot_general(a, left_zero[...], NT, preferred_element_type=F32)
            m = masks[k : k + 1]
            for i in range(16):
                x = x0 + i
                s = jnp.where(lane <= x, hi[i * G : i * G + G], lo[i * G : i * G + G])
                if x < ndisp - 1:
                    s = pltpu.roll(s, ndisp - 1 - x, 1)
                put(x + 2, s * m)

        mask_n = xn[2 * cols : 2 * cols + 16, :].astype(F32)
        tail = xn[cols - 16 : cols, :].astype(F32)[14:16]
        head = xn[0:16, :].astype(F32)[0:2]
        a = spread(jnp.concatenate([tail, head], axis=0))
        p_n = lax.dot_general(a, xn[right, :], NT, preferred_element_type=F32)
        p_o = lax.dot_general(a, xs[right, :], NT, preferred_element_type=F32)
        m_l = jnp.where(is_left, 0.0, mask_n[15:16])
        m_r = jnp.where(is_right, 0.0, mask_n[0:1])
        s = jnp.where(lane <= ndisp - 2, p_n[0:G], 0.0)
        put(0, pltpu.roll(s, 1, 1) * m_l)
        put(1, p_n[G : 2 * G] * m_l)
        s = jnp.where(lane <= 0, p_n[2 * G : 3 * G], p_o[2 * G : 3 * G])
        put(cols + 2, pltpu.roll(s, ndisp - 1, 1) * m_r)
        s = jnp.where(lane <= 1, p_n[3 * G : 4 * G], p_o[3 * G : 4 * G])
        put(cols + 3, pltpu.roll(s, ndisp - 2, 1) * m_r)


def row_block(refs, span):
    data = jnp.concatenate([ref[span] for ref in refs], axis=1)
    return data.reshape(data.shape[0] * data.shape[1], data.shape[2])


def first_conv(w_own, w_other, own, other, hidden):
    def step(s, carry):
        span = pl.ds(s * STEP1, STEP1 + 2)
        h = jnp.dot(w_own, row_block(own, span), preferred_element_type=F32)
        h += jnp.dot(w_other, row_block(other, span), preferred_element_type=F32)
        h = jnp.maximum(h, 0.0).astype(BF)
        hidden[pl.ds(s * STEP1, STEP1)] = h.reshape(STEP1, PAIR, h.shape[1])
        return carry

    lax.fori_loop(0, hidden.shape[0] // STEP1, step, 0, unroll=True)


def clear_rim(ref, outside, cols):
    is_left, is_right, _, _, _ = place()
    ndisp = ref.shape[2]
    for which in (0, 1):
        @pl.when(outside[which])
        def _():
            def clear(i, carry):
                ref[i, which * G : which * G + G, :] = jnp.zeros((G, ndisp), BF)
                return carry

            lax.fori_loop(0, cols + 2, clear, 0, unroll=8)

    for flag, col in ((is_left, 0), (is_right, cols + 1)):
        @pl.when(flag)
        def _():
            ref[col] = jnp.zeros((PAIR, ndisp), BF)


def tap_row(weights, order, width):
    pieces = []
    for j in range(3):
        for i in order:
            pieces.append(jnp.zeros((G, G), F32) if i is None else weights[i, j].astype(F32))
    pieces.append(jnp.zeros((G, width - 3 * len(order) * G), F32))
    return jnp.concatenate(pieces, axis=1)


def moved(line, by):
    return (pltpu.roll(line, by, 1) if by else line).astype(BF)


def permuted_columns(matrix, source):
    order = jnp.where(iota(source.shape, 0) == source, 1.0, 0.0).astype(BF)
    return jnp.dot(matrix, order, preferred_element_type=F32).astype(BF)


def weights_kernel(s1, s2, taps, w1, w2, tm):
    ndisp = tm.shape[1]
    depth = (STEP1 + 2) * 4 * G
    line = tap_row(s1, (0, 1, 2, None), depth)
    plain = [moved(line, (xo * 4 + yo) * G) for xo in range(STEP1) for yo in range(2)]
    c = iota((depth, depth), 1)
    half = depth // 2
    source = ((c % half) // PAIR) * (2 * PAIR) + (c // half) * PAIR + c % PAIR
    sorted_cols = permuted_columns(jnp.concatenate(plain, axis=0), source)
    w1[0] = sorted_cols[:, :half]
    w1[1] = sorted_cols[:, half:]

    size = STEP2 * G
    r = iota((size, size), 0)
    source = (r % STEP2) * G + r // STEP2
    order = jnp.where(iota((size, size), 1) == source, 1.0, 0.0).astype(BF)
    for v, taps_order in enumerate(((0, 1, 2), (1, 2, 0), (2, 0, 1))):
        line = tap_row(s2, taps_order, w2.shape[2])
        plain = jnp.concatenate([moved(line, xo * 3 * G) for xo in range(STEP2)], axis=0)
        w2[v] = jnp.dot(order, plain, preferred_element_type=F32).astype(BF)

    k = iota((TAPS, ndisp), 0)
    at = iota((TAPS, ndisp), 1)
    spot = TAPS // 2 - k
    spot = jnp.where(spot < 0, spot + ndisp, spot)
    spot = jnp.where(at == spot, 1.0, 0.0).astype(BF)
    lines = jnp.dot(taps[...], spot, preferred_element_type=F32)
    r = iota((ndisp, ndisp), 0)
    c = iota((ndisp, ndisp), 1)
    flip = jnp.where(r + c == ndisp - 1, 1.0, 0.0).astype(BF)
    inside = jnp.abs(r - c) <= TAPS // 2
    for g in range(G):
        line = jnp.broadcast_to(lines[g : g + 1, :], (ndisp, ndisp))
        line = pltpu.roll(line, 0, 1, stride=1, stride_axis=0)
        line = jnp.where(inside, line, 0.0).astype(BF)
        tm[g * ndisp : (g + 1) * ndisp, :] = jnp.dot(
            flip, line, preferred_element_type=F32
        ).astype(BF)


def own_kernel(own0, own1, own0_n, own1_n, o0, o1, left_zero):
    correlate(((own0, own0_n, o0), (own1, own1_n, o1)), left_zero)


def partner_kernel(par0, par1, par0_n, par1_n, o0, o1, w1, hidden, left_zero, p0, p1):
    _, _, first, last, odd = place()
    correlate(((par0, par0_n, p0), (par1, par1_n, p1)), left_zero)
    first_conv(w1[odd], w1[1 - odd], (o0, o1), (p0, p1), hidden)
    clear_rim(hidden, ((odd == 1) & first, (odd == 0) & last), left_zero.shape[0])


def row_kernel(xs, xn, corr, left_zero):
    correlate(((xs, xn, corr),), left_zero)


def last_kernel(
    far1, far1_n, f0, o0, o1, partner, w1, w2, tm, out_ref, left_zero, f1, hidden, second
):
    _, _, first, last, odd = place()
    cols = left_zero.shape[0]
    ndisp = tm.shape[1]
    correlate(((far1, far1_n, f1),), left_zero)
    first_conv(w1[1 - odd], w1[odd], (o0, o1), (f0, f1), hidden)
    clear_rim(hidden, ((odd == 0) & first, (odd == 1) & last), cols)
    one = pl.ds(pl.multiple_of(odd * G, G), G)
    other = pl.ds(pl.multiple_of((1 - odd) * G, G), G)
    outputs = ((odd, w2[odd]), (1 - odd, w2[2 * odd]))

    def next_hidden(u, carry):
        halves = ([], [])
        for v in range(2):
            span = pl.ds((2 * u + v) * STEP2, STEP2 + 2)
            blocks = ((hidden[span], partner[span, one, :]), (hidden[span, other, :], partner[span]))
            for half, block, (_, weights) in zip(halves, blocks, outputs):
                data = jnp.concatenate(block, axis=1).reshape((STEP2 + 2) * 3 * G, ndisp)
                h = jnp.dot(weights, data, preferred_element_type=F32)
                half.append(jnp.maximum(h, 0.0))
        for half, (y, _) in zip(halves, outputs):
            for o in range(G):
                r = o * STEP2
                both = jnp.concatenate([h[r : r + STEP2] for h in half], axis=0)
                second[y, pl.ds(pl.multiple_of(u * 16, 16), 16), o * ndisp : (o + 1) * ndisp] = (
                    both.astype(BF)
                )
        return carry

    lax.fori_loop(0, cols // 16, next_hidden, 0, unroll=True)

    for y in range(2):
        out_ref[y] = jnp.dot(second[y], tm[...], preferred_element_type=F32)


def body(
    left_feat, right_feat, block_list, block_count, spatial_first, spatial_second, disparity_weight
):
    row_count, cols, channels = left_feat.shape
    ndisp = NBLK * DB
    bands = lax.axis_size("rows")
    row = lax.axis_index("rows")
    packed = jax.ShapeDtypeStruct((2 * cols + 16, channels), BF)
    lists = block_list.transpose(0, 2, 1)
    chunks = [
        pl.pallas_call(
            functools.partial(pack_kernel, c),
            out_shape=packed,
            in_specs=[HBM, HBM, SMEM, SMEM],
            out_specs=VMEM,
            scratch_shapes=[pltpu.SemaphoreType.DMA((2,))],
            cost_estimate=cost(1),
        )(left_feat, right_feat, lists, block_count)
        for c in range(row_count)
    ]

    partners = [(i, i ^ 1) for i in range(bands) if i ^ 1 < bands]
    onward = [(i, i + 2 - 4 * (i % 2)) for i in range(bands)]
    onward = [(i, j) for i, j in onward if 0 <= j < bands]
    across = [(0, 1), (1, 0)]

    def cross(x):
        return lax.ppermute(x, "cols", across)

    par0, par1 = [lax.ppermute(x, "rows", partners) for x in chunks]
    own_n = [cross(x) for x in chunks]
    steps1 = -(-(cols + 2) // STEP1)
    depth1 = (STEP1 + 2) * PAIR
    depth2 = (STEP2 + 2) * 3 * G
    volume = (steps1 * STEP1 + 2, G, ndisp)
    volume_out = jax.ShapeDtypeStruct(volume, BF)
    pair = (steps1 * STEP1, PAIR, ndisp)
    left_zero = pltpu.VMEM((cols, channels), BF)

    w1, w2, tm = pl.pallas_call(
        weights_kernel,
        out_shape=[
            jax.ShapeDtypeStruct((2, STEP1 * PAIR, depth1), BF),
            jax.ShapeDtypeStruct((3, STEP2 * G, depth2), BF),
            jax.ShapeDtypeStruct((G * ndisp, ndisp), BF),
        ],
        in_specs=[VMEM] * 3,
        out_specs=[VMEM] * 3,
        compiler_params=LIMIT,
        cost_estimate=cost(4),
    )(spatial_first, spatial_second, disparity_weight.T)

    o0, o1 = pl.pallas_call(
        own_kernel,
        out_shape=[volume_out] * 2,
        in_specs=[VMEM] * 4,
        out_specs=[VMEM] * 2,
        scratch_shapes=[left_zero],
        compiler_params=LIMIT,
        cost_estimate=cost(4),
    )(*chunks, *own_n)
    par0, w1, o0 = lax.optimization_barrier((par0, w1, o0))
    if bands % 2:
        onward.append((bands - 1, bands - 2))

    def send_on(chunk, x):
        if bands % 2:
            x = jnp.where(row == bands - 1, chunk, x)
        return lax.ppermute(x, "rows", onward)

    far0 = send_on(chunks[0], par0)
    par0_n = cross(par0)

    far1 = send_on(chunks[1], par1)
    par1_n = cross(par1)
    par1_n, far0 = lax.optimization_barrier((par1_n, far0))

    hidden = pl.pallas_call(
        partner_kernel,
        out_shape=jax.ShapeDtypeStruct(pair, BF),
        in_specs=[VMEM] * 7,
        out_specs=VMEM,
        scratch_shapes=[left_zero, pltpu.VMEM(volume, BF), pltpu.VMEM(volume, BF)],
        compiler_params=LIMIT,
        cost_estimate=cost(8),
    )(par0, par1, par0_n, par1_n, o0, o1, w1)
    far0_n = cross(far0)
    far1, hidden = lax.optimization_barrier((far1, hidden))
    f0 = pl.pallas_call(
        row_kernel,
        out_shape=volume_out,
        in_specs=[VMEM] * 2,
        out_specs=VMEM,
        scratch_shapes=[left_zero],
        compiler_params=LIMIT,
        cost_estimate=cost(1),
    )(far0, far0_n)

    return pl.pallas_call(
        last_kernel,
        out_shape=jax.ShapeDtypeStruct((row_count, cols, ndisp), F32),
        in_specs=[VMEM] * 9,
        out_specs=VMEM,
        scratch_shapes=[
            left_zero,
            pltpu.VMEM(volume, BF),
            pltpu.VMEM(pair, BF),
            pltpu.VMEM((2, cols, G * ndisp), BF),
        ],
        compiler_params=LIMIT,
        cost_estimate=cost(12),
    )(far1, cross(far1), f0, o0, o1, hidden, w1, w2, tm)


def solution(mesh):
    in_specs = (
        P(("pairs", "rows"), "cols", None),
        P(("pairs", "rows"), "cols", None),
        P(("pairs", "rows"), "cols", None),
        P(("pairs", "rows"), "cols"),
        P(),
        P(),
        P(),
    )
    out_specs = P(("pairs", "rows"), "cols", None)
    return jax.shard_map(body, mesh=mesh, in_specs=in_specs, out_specs=out_specs, check_vma=False)
```

```python
import functools

import jax
import jax.numpy as jnp
from jax import lax
from jax.experimental import pallas as pl
from jax.experimental.pallas import tpu as pltpu
from jax.sharding import PartitionSpec as P

G = 16
DB = 128
NBLK = 2
TILE = 64
TAPS = 17
STEP1 = 6
STEP2 = 8
PAIR = 2 * G
BF = jnp.bfloat16
F32 = jnp.float32
NT = (((1,), (1,)), ((), ()))
VMEM = pl.BlockSpec(memory_space=pltpu.VMEM)
SMEM = pl.BlockSpec(memory_space=pltpu.SMEM)
HBM = pl.BlockSpec(memory_space=pl.ANY)
LIMIT = pltpu.CompilerParams(vmem_limit_bytes=36 * 1024 * 1024)


def cost(us):
    return pl.CostEstimate(flops=us * 10**9, bytes_accessed=us * 10**6, transcendentals=0)


def iota(shape, dim):
    return lax.broadcasted_iota(jnp.int32, shape, dim)


def place():
    row, col = lax.axis_index("rows"), lax.axis_index("cols")
    rows, cols = lax.axis_size("rows"), lax.axis_size("cols")
    return col == 0, col == cols - 1, row == 0, row == rows - 1, row % 2


def pack_kernel(c, left, right, block_list, block_count, pack, sems):
    cols = left.shape[1]
    copies = []
    for i, src in enumerate((left, right)):
        dst = pack.at[pl.ds(i * cols, cols), :]
        copies.append(pltpu.make_async_copy(src.at[c], dst, sems.at[i]))
        copies[-1].start()
    ndisp = pack.shape[1]
    lane_block = (ndisp - 1 - iota((TILE // 16, ndisp), 1)) // DB
    lines = []
    for tile in range(cols // TILE):
        line = jnp.zeros(lane_block.shape, F32)
        for slot in range(block_list.shape[1]):
            listed = jnp.where(slot < block_count[0, tile], block_list[0, slot, tile], -1)
            line = jnp.where(lane_block == listed, 1.0, line)
        lines.append(line)
    pack[2 * cols :, :] = jnp.concatenate(lines, axis=0).astype(BF)
    for copy in copies:
        copy.wait()


def correlate(rows, left_zero):
    is_left, is_right, _, _, _ = place()
    cols, channels = left_zero.shape
    ndisp = NBLK * DB
    group_of = iota((G, channels), 1) // (channels // G)
    gmask = jnp.where(group_of == iota((G, channels), 0), (channels // G) ** -0.5, 0.0).astype(F32)
    lane = iota((G, ndisp), 1)

    def spread(lines):
        lines = lines.astype(F32)
        return jnp.concatenate(
            [(lines[i : i + 1, :] * gmask).astype(BF) for i in range(lines.shape[0])], axis=0
        )

    for xs, xn, corr in rows:

        def put(xx, value, corr=corr):
            corr[xx] = value.astype(BF)

        right = slice(cols, 2 * cols)
        near = xn[right, :]
        left_zero[...] = jnp.where(is_left, jnp.zeros_like(near), near)
        masks = xs[2 * cols : 2 * cols + 16, :].astype(F32)
        for k in range(cols // 16):
            x0 = k * 16
            a = spread(xs[x0 : x0 + 16, :])
            hi = lax.dot_general(a, xs[right, :], NT, preferred_element_type=F32)
            lo = lax.dot_general(a, left_zero[...], NT, preferred_element_type=F32)
            m = masks[k : k + 1].astype(BF)
            for i in range(16):
                x = x0 + i
                s = jnp.where(lane <= x, hi[i * G : i * G + G], lo[i * G : i * G + G])
                if x < ndisp - 1:
                    s = pltpu.roll(s, ndisp - 1 - x, 1)
                put(x + 2, s.astype(BF) * m)

        mask_n = xn[2 * cols : 2 * cols + 16, :].astype(F32)
        tail = xn[cols - 16 : cols, :].astype(F32)[14:16]
        head = xn[0:16, :].astype(F32)[0:2]
        a = spread(jnp.concatenate([tail, head], axis=0))
        p_n = lax.dot_general(a, xn[right, :], NT, preferred_element_type=F32)
        p_o = lax.dot_general(a, xs[right, :], NT, preferred_element_type=F32)
        m_l = jnp.where(is_left, 0.0, mask_n[15:16])
        m_r = jnp.where(is_right, 0.0, mask_n[0:1])
        s = jnp.where(lane <= ndisp - 2, p_n[0:G], 0.0)
        put(0, pltpu.roll(s, 1, 1) * m_l)
        put(1, p_n[G : 2 * G] * m_l)
        s = jnp.where(lane <= 0, p_n[2 * G : 3 * G], p_o[2 * G : 3 * G])
        put(cols + 2, pltpu.roll(s, ndisp - 1, 1) * m_r)
        s = jnp.where(lane <= 1, p_n[3 * G : 4 * G], p_o[3 * G : 4 * G])
        put(cols + 3, pltpu.roll(s, ndisp - 2, 1) * m_r)


def row_block(refs, span):
    data = jnp.concatenate([ref[span] for ref in refs], axis=1)
    return data.reshape(data.shape[0] * data.shape[1], data.shape[2])


def first_conv(w_own, w_other, own, other, hidden):
    def step(s, carry):
        span = pl.ds(s * STEP1, STEP1 + 2)
        h = jnp.dot(w_own, row_block(own, span), preferred_element_type=F32)
        h += jnp.dot(w_other, row_block(other, span), preferred_element_type=F32)
        h = jnp.maximum(h, 0.0).astype(BF)
        hidden[pl.ds(s * STEP1, STEP1)] = h.reshape(STEP1, PAIR, h.shape[1])
        return carry

    lax.fori_loop(0, hidden.shape[0] // STEP1, step, 0, unroll=True)


def clear_rim(ref, outside, cols):
    is_left, is_right, _, _, _ = place()
    ndisp = ref.shape[2]
    for which in (0, 1):
        @pl.when(outside[which])
        def _():
            def clear(i, carry):
                ref[i, which * G : which * G + G, :] = jnp.zeros((G, ndisp), BF)
                return carry

            lax.fori_loop(0, cols + 2, clear, 0, unroll=8)

    for flag, col in ((is_left, 0), (is_right, cols + 1)):
        @pl.when(flag)
        def _():
            ref[col] = jnp.zeros((PAIR, ndisp), BF)


def tap_row(weights, order, width):
    pieces = []
    for j in range(3):
        for i in order:
            pieces.append(jnp.zeros((G, G), F32) if i is None else weights[i, j].astype(F32))
    pieces.append(jnp.zeros((G, width - 3 * len(order) * G), F32))
    return jnp.concatenate(pieces, axis=1)


def moved(line, by):
    return (pltpu.roll(line, by, 1) if by else line).astype(BF)


def permuted_columns(matrix, source):
    order = jnp.where(iota(source.shape, 0) == source, 1.0, 0.0).astype(BF)
    return jnp.dot(matrix, order, preferred_element_type=F32).astype(BF)


def weights_kernel(s1, s2, taps, w1, w2, tm):
    ndisp = tm.shape[1]
    depth = (STEP1 + 2) * 4 * G
    line = tap_row(s1, (0, 1, 2, None), depth)
    plain = [moved(line, (xo * 4 + yo) * G) for xo in range(STEP1) for yo in range(2)]
    c = iota((depth, depth), 1)
    half = depth // 2
    source = ((c % half) // PAIR) * (2 * PAIR) + (c // half) * PAIR + c % PAIR
    sorted_cols = permuted_columns(jnp.concatenate(plain, axis=0), source)
    w1[0] = sorted_cols[:, :half]
    w1[1] = sorted_cols[:, half:]

    size = STEP2 * G
    r = iota((size, size), 0)
    source = (r % STEP2) * G + r // STEP2
    order = jnp.where(iota((size, size), 1) == source, 1.0, 0.0).astype(BF)
    for v, taps_order in enumerate(((0, 1, 2), (1, 2, 0), (2, 0, 1))):
        line = tap_row(s2, taps_order, w2.shape[2])
        plain = jnp.concatenate([moved(line, xo * 3 * G) for xo in range(STEP2)], axis=0)
        w2[v] = jnp.dot(order, plain, preferred_element_type=F32).astype(BF)

    k = iota((TAPS, ndisp), 0)
    at = iota((TAPS, ndisp), 1)
    spot = TAPS // 2 - k
    spot = jnp.where(spot < 0, spot + ndisp, spot)
    spot = jnp.where(at == spot, 1.0, 0.0).astype(BF)
    lines = jnp.dot(taps[...], spot, preferred_element_type=F32)
    r = iota((ndisp, ndisp), 0)
    c = iota((ndisp, ndisp), 1)
    flip = jnp.where(r + c == ndisp - 1, 1.0, 0.0).astype(BF)
    inside = jnp.abs(r - c) <= TAPS // 2
    for g in range(G):
        line = jnp.broadcast_to(lines[g : g + 1, :], (ndisp, ndisp))
        line = pltpu.roll(line, 0, 1, stride=1, stride_axis=0)
        line = jnp.where(inside, line, 0.0).astype(BF)
        tm[g * ndisp : (g + 1) * ndisp, :] = jnp.dot(
            flip, line, preferred_element_type=F32
        ).astype(BF)


def own_kernel(own0, own1, own0_n, own1_n, o0, o1, left_zero):
    correlate(((own0, own0_n, o0), (own1, own1_n, o1)), left_zero)


def partner_kernel(par0, par1, par0_n, par1_n, o0, o1, w1, hidden, left_zero, p0, p1):
    _, _, first, last, odd = place()
    correlate(((par0, par0_n, p0), (par1, par1_n, p1)), left_zero)
    first_conv(w1[odd], w1[1 - odd], (o0, o1), (p0, p1), hidden)
    clear_rim(hidden, ((odd == 1) & first, (odd == 0) & last), left_zero.shape[0])


def row_kernel(xs, xn, corr, left_zero):
    correlate(((xs, xn, corr),), left_zero)


def last_kernel(
    far1, far1_n, f0, o0, o1, partner, w1, w2, tm, out_ref, left_zero, f1, hidden, second
):
    _, _, first, last, odd = place()
    cols = left_zero.shape[0]
    ndisp = tm.shape[1]
    correlate(((far1, far1_n, f1),), left_zero)
    first_conv(w1[1 - odd], w1[odd], (o0, o1), (f0, f1), hidden)
    clear_rim(hidden, ((odd == 0) & first, (odd == 1) & last), cols)
    one = pl.ds(pl.multiple_of(odd * G, G), G)
    other = pl.ds(pl.multiple_of((1 - odd) * G, G), G)
    outputs = ((odd, w2[odd]), (1 - odd, w2[2 * odd]))

    def next_hidden(u, carry):
        halves = ([], [])
        for v in range(2):
            span = pl.ds((2 * u + v) * STEP2, STEP2 + 2)
            blocks = ((hidden[span], partner[span, one, :]), (hidden[span, other, :], partner[span]))
            for half, block, (_, weights) in zip(halves, blocks, outputs):
                data = jnp.concatenate(block, axis=1).reshape((STEP2 + 2) * 3 * G, ndisp)
                h = jnp.dot(weights, data, preferred_element_type=F32)
                half.append(jnp.maximum(h, 0.0))
        for half, (y, _) in zip(halves, outputs):
            for o in range(G):
                r = o * STEP2
                both = jnp.concatenate([h[r : r + STEP2] for h in half], axis=0)
                second[y, pl.ds(pl.multiple_of(u * 16, 16), 16), o * ndisp : (o + 1) * ndisp] = (
                    both.astype(BF)
                )
        return carry

    lax.fori_loop(0, cols // 16, next_hidden, 0, unroll=True)

    for y in range(2):
        out_ref[y] = jnp.dot(second[y], tm[...], preferred_element_type=F32)


def body(
    left_feat, right_feat, block_list, block_count, spatial_first, spatial_second, disparity_weight
):
    row_count, cols, channels = left_feat.shape
    ndisp = NBLK * DB
    bands = lax.axis_size("rows")
    row = lax.axis_index("rows")
    packed = jax.ShapeDtypeStruct((2 * cols + 16, channels), BF)
    lists = block_list.transpose(0, 2, 1)
    chunks = [
        pl.pallas_call(
            functools.partial(pack_kernel, c),
            out_shape=packed,
            in_specs=[HBM, HBM, SMEM, SMEM],
            out_specs=VMEM,
            scratch_shapes=[pltpu.SemaphoreType.DMA((2,))],
            cost_estimate=cost(1),
        )(left_feat, right_feat, lists, block_count)
        for c in range(row_count)
    ]

    partners = [(i, i ^ 1) for i in range(bands) if i ^ 1 < bands]
    onward = [(i, i + 2 - 4 * (i % 2)) for i in range(bands)]
    onward = [(i, j) for i, j in onward if 0 <= j < bands]
    across = [(0, 1), (1, 0)]

    def cross(x):
        return lax.ppermute(x, "cols", across)

    par0, par1 = [lax.ppermute(x, "rows", partners) for x in chunks]
    own_n = [cross(x) for x in chunks]
    steps1 = -(-(cols + 2) // STEP1)
    depth1 = (STEP1 + 2) * PAIR
    depth2 = (STEP2 + 2) * 3 * G
    volume = (steps1 * STEP1 + 2, G, ndisp)
    volume_out = jax.ShapeDtypeStruct(volume, BF)
    pair = (steps1 * STEP1, PAIR, ndisp)
    left_zero = pltpu.VMEM((cols, channels), BF)

    w1, w2, tm = pl.pallas_call(
        weights_kernel,
        out_shape=[
            jax.ShapeDtypeStruct((2, STEP1 * PAIR, depth1), BF),
            jax.ShapeDtypeStruct((3, STEP2 * G, depth2), BF),
            jax.ShapeDtypeStruct((G * ndisp, ndisp), BF),
        ],
        in_specs=[VMEM] * 3,
        out_specs=[VMEM] * 3,
        compiler_params=LIMIT,
        cost_estimate=cost(4),
    )(spatial_first, spatial_second, disparity_weight.T)

    o0, o1 = pl.pallas_call(
        own_kernel,
        out_shape=[volume_out] * 2,
        in_specs=[VMEM] * 4,
        out_specs=[VMEM] * 2,
        scratch_shapes=[left_zero],
        compiler_params=LIMIT,
        cost_estimate=cost(4),
    )(*chunks, *own_n)
    par0, w1, o0 = lax.optimization_barrier((par0, w1, o0))
    if bands % 2:
        onward.append((bands - 1, bands - 2))

    def send_on(chunk, x):
        if bands % 2:
            x = jnp.where(row == bands - 1, chunk, x)
        return lax.ppermute(x, "rows", onward)

    far0 = send_on(chunks[0], par0)
    par0_n = cross(par0)

    far1 = send_on(chunks[1], par1)
    par1_n = cross(par1)
    par1_n, far0 = lax.optimization_barrier((par1_n, far0))

    hidden = pl.pallas_call(
        partner_kernel,
        out_shape=jax.ShapeDtypeStruct(pair, BF),
        in_specs=[VMEM] * 7,
        out_specs=VMEM,
        scratch_shapes=[left_zero, pltpu.VMEM(volume, BF), pltpu.VMEM(volume, BF)],
        compiler_params=LIMIT,
        cost_estimate=cost(8),
    )(par0, par1, par0_n, par1_n, o0, o1, w1)
    far0_n = cross(far0)
    far1, hidden = lax.optimization_barrier((far1, hidden))
    f0 = pl.pallas_call(
        row_kernel,
        out_shape=volume_out,
        in_specs=[VMEM] * 2,
        out_specs=VMEM,
        scratch_shapes=[left_zero],
        compiler_params=LIMIT,
        cost_estimate=cost(1),
    )(far0, far0_n)

    return pl.pallas_call(
        last_kernel,
        out_shape=jax.ShapeDtypeStruct((row_count, cols, ndisp), F32),
        in_specs=[VMEM] * 9,
        out_specs=VMEM,
        scratch_shapes=[
            left_zero,
            pltpu.VMEM(volume, BF),
            pltpu.VMEM(pair, BF),
            pltpu.VMEM((2, cols, G * ndisp), BF),
        ],
        compiler_params=LIMIT,
        cost_estimate=cost(12),
    )(far1, cross(far1), f0, o0, o1, hidden, w1, w2, tm)


def solution(mesh):
    in_specs = (
        P(("pairs", "rows"), "cols", None),
        P(("pairs", "rows"), "cols", None),
        P(("pairs", "rows"), "cols", None),
        P(("pairs", "rows"), "cols"),
        P(),
        P(),
        P(),
    )
    out_specs = P(("pairs", "rows"), "cols", None)
    return jax.shard_map(body, mesh=mesh, in_specs=in_specs, out_specs=out_specs, check_vma=False)
```
